32 devices in a mesh: alpha: 8 (over y, x, core), beta: 4 (over z).
Axes of the slice: x: 2, y: 2, z: 4, core: 2. Of those that a mesh axis runs over, the one named last changes fastest.
Arguments:
- coeffs: float32 [4096, 8192], P('alpha', 'beta'), may hold values from -6 to 6
- diag_alpha: float32 [4096], P('alpha'), may hold values from 0.5 to 2
- diag_beta: float32 [8192], P('beta'), may hold values from 0.5 to 2
- alpha_tiles: float32 [16, 8, 256, 256], P('alpha'), may hold values from -0.375 to 0.375
- beta_hamiltonian_tiles: float32 [32, 8, 256, 256], P('beta'), may hold values from -0.375 to 0.375
- alpha_source: int32 [16, 8], replicated, may hold values from 0 to 15, as said below
- alpha_live: int32 [16, 8], replicated, may hold values from 0 to 1, as said below
- beta_source_block: int32 [32, 8], replicated, may hold values from 0 to 31, as said below
- beta_live: int32 [32, 8], replicated, may hold values from 0 to 1, as said below
Outputs:
- sigma: float32 [4096, 8192], P('alpha', 'beta')
The draws below stay inside these ranges and needn't reach their ends.
Inputs may be any that keep to these rules, and one draw needn't show every extreme that they name: `beta_source_block`: target blocks are grouped by device: the 32 / 4 consecutive target blocks of one beta index ask, over all their slots, exactly (32 // 4 * 8) // 4 source blocks (counted with repetition) of every beta index, where beta index k holds blocks k * (32 // 4) onward. `alpha_source`: likewise for alpha: the 2 consecutive target blocks of one alpha index ask, over all their slots, exactly 2 * 8 // 8 source blocks of every alpha index. `beta_live`: in each target block the live slots come first, and slot 0 is live. `alpha_live`: in each target block the live slots come first, and slot 0 is live.
All inputs are finite; a program needn't handle non-finite values.
Results may differ from the reference program's by a relative error of at most 0.0003.
Values sent between devices are 32-bit elements; how exact they have to be, the bound alone decides.
A program may use at most 192 MiB of HBM per device.

```python
import jax
import jax.numpy as jnp
from jax import lax

BS = 256
NCPL = 8
NB = 8192
NA = 4096
NAB = 16
NBB = 32
N_ALPHA = 8
N_BETA = 4


def coupling_table(key, block_total, devices):
    blocks_dev = block_total // devices
    requests = blocks_dev * NCPL
    processor_random_keys = jax.random.split(key, devices)

    def per_device(device_key):
        perm_key, inner_key = jax.random.split(device_key)
        owners = jax.random.permutation(perm_key, requests) % devices
        inner_identifiers = jax.random.randint(inner_key, (requests,), 0, blocks_dev)
        return owners * blocks_dev + inner_identifiers
    coupled = jax.vmap(per_device)(processor_random_keys)
    return coupled.reshape(block_total, NCPL).astype(jnp.int32)


def live_table(key, block_total):
    counts_live = jax.random.randint(key, (block_total,), 1, NCPL + 1)
    slot_ids = jnp.arange(NCPL)
    return (slot_ids[None, :] < counts_live[:, None]).astype(jnp.int32)


def draw_alpha_source(key, part):
    return coupling_table(jax.random.fold_in(key, 11), NA // BS, N_ALPHA)


def draw_beta_source_block(key, part):
    return coupling_table(jax.random.fold_in(key, 23), NB // BS, N_BETA)


def draw_alpha_live(key, part):
    return live_table(jax.random.fold_in(key, 37), NA // BS)


def draw_beta_live(key, part):
    return live_table(jax.random.fold_in(key, 41), NB // BS)


def levels(stream_key, dims, shards, low, top_value):
    loudness = 1.0
    for axis_at, shards_of in shards:
        steps = jax.random.uniform(jax.random.fold_in(jax.random.fold_in(stream_key, 6), axis_at), (shards_of,), jnp.float32, low / len(shards), top_value / len(shards))
        loudness = loudness * jnp.repeat(jnp.exp(steps), dims[axis_at] // shards_of).reshape((-1,) + (1,) * (len(dims) - 1 - axis_at))
    return loudness


def normal_values(stream_key, dims, spread, most, cuts=(), dtype=jnp.bfloat16):
    array = jax.random.normal(stream_key, dims, jnp.float32) * spread
    if len(cuts) > 0:
        array = levels(stream_key, dims, cuts, -0.22, 0.18) * array
    return jnp.clip(array, min=-most, max=most).astype(dtype)


def setup_inputs(seed: int = 0) -> dict:
    key_of = jax.random.split(jax.random.key(seed), 10)
    return {
        "coeffs": normal_values(key_of[0], (NA, NB), 1.0, 6.0, ((0, 8), (1, 4)), jnp.float32),
        "diag_alpha": jnp.clip(0.5 + 1.5 * jax.random.uniform(key_of[1], (NA,), jnp.float32) ** levels(key_of[1], (NA,), ((0, 8),), -0.2, 0.2), 0.5, 2.0),
        "diag_beta": jnp.clip(0.5 + 1.5 * jax.random.uniform(key_of[2], (NB,), jnp.float32) ** levels(key_of[2], (NB,), ((0, 4),), -0.2, 0.2), 0.5, 2.0),
        "alpha_tiles": normal_values(key_of[3], (NAB, NCPL, BS, BS), BS ** -0.5, 0.375, ((0, 8),), jnp.float32),
        "beta_hamiltonian_tiles": normal_values(key_of[4], (NBB, NCPL, BS, BS), BS ** -0.5, 0.375, ((0, 4),), jnp.float32),
        "alpha_source": draw_alpha_source(jax.random.fold_in(key_of[9], 71), 0),
        "alpha_live": draw_alpha_live(jax.random.fold_in(key_of[9], 71), 0),
        "beta_source_block": draw_beta_source_block(jax.random.fold_in(key_of[9], 71), 0),
        "beta_live": draw_beta_live(jax.random.fold_in(key_of[9], 71), 0),
    }


def beta_pass(coeffs, beta_hamiltonian_tiles, beta_source_block, beta_live):
    rows_all = coeffs.shape[0]
    block_size = beta_hamiltonian_tiles.shape[2]
    block_total = beta_hamiltonian_tiles.shape[0]
    blocks = coeffs.reshape(rows_all, block_total, block_size)

    def one_target(packed):
        tile_set, sources, flags = packed
        picked = jnp.take(blocks, sources.astype(jnp.int32), axis=1)
        masked = tile_set * flags.astype(jnp.float32)[:, None, None]
        return jnp.einsum("acb,cbd->ad", picked, masked, precision=lax.Precision.HIGHEST)

    sigma_output = lax.map(one_target, (beta_hamiltonian_tiles, beta_source_block, beta_live))
    return jnp.transpose(sigma_output, (1, 0, 2)).reshape(rows_all, block_total * block_size)


def alpha_pass(coeffs, alpha_tiles, alpha_source, alpha_live):
    cols_all = coeffs.shape[1]
    block_size = alpha_tiles.shape[2]
    block_total = alpha_tiles.shape[0]
    blocks = coeffs.reshape(block_total, block_size, cols_all)

    def one_target(packed):
        tile_set, sources, flags = packed
        picked = jnp.take(blocks, sources.astype(jnp.int32), axis=0)
        masked = tile_set * flags.astype(jnp.float32)[:, None, None]
        return jnp.einsum("cab,cbd->ad", masked, picked, precision=lax.Precision.HIGHEST)

    sigma_output = lax.map(one_target, (alpha_tiles, alpha_source, alpha_live))
    return sigma_output.reshape(block_total * block_size, cols_all)


def reference(coeffs, diag_alpha, diag_beta, alpha_tiles, beta_hamiltonian_tiles, alpha_source, alpha_live, beta_source_block, beta_live):
    beta_term = beta_pass(coeffs, beta_hamiltonian_tiles, beta_source_block, beta_live)
    alpha_term = alpha_pass(coeffs, alpha_tiles, alpha_source, alpha_live)
    diagonal = diag_alpha[:, None] + diag_beta[None, :]
    return diagonal * coeffs + beta_term + alpha_term
```

```python
import functools

import jax
import jax.numpy as jnp
from jax import lax
from jax.experimental import pallas as pl
from jax.experimental.pallas import tpu as pltpu
from jax.sharding import PartitionSpec as P

HALVES = 2
VMEM_LIMIT = 48 * 1024 * 1024


def split(x):
    high = x.astype(jnp.bfloat16)
    low = (x - high.astype(jnp.float32)).astype(jnp.bfloat16)
    return high, low


def product(a, b):
    a_high, a_low = a
    b_high, b_low = b
    dot = functools.partial(jnp.dot, preferred_element_type=jnp.float32)
    return dot(a_high, b_high) + (dot(a_high, b_low) + dot(a_low, b_high))


def beta_kernel(couplings, count, first, source, live, place, *refs):
    if first:
        tiles, da, db, own, out = refs
        buffers = (own,)
    else:
        tiles, left, right, total, out = refs
        buffers = (left, right)
    size = tiles.shape[-1]
    me, step = place[0], place[1]
    target = pl.program_id(0)
    if first:
        columns = pl.ds(pl.multiple_of(target * size, size), size)
        out[...] = (da[...] + db[:, columns]) * own[:, columns]
    else:
        out[...] = total[...]
    owners = (me,) if first else (me - step, me + step)

    def slot(c, carry):
        at = (me * count + target) * couplings + c
        block = source[at]
        owner = block // count
        inner = block - owner * count
        columns = pl.ds(pl.multiple_of(inner * size, size), size)
        for buffer, wanted in zip(buffers, owners):

            @pl.when(jnp.logical_and(live[at] != 0, owner == wanted))
            def _():
                out[...] += product(split(buffer[:, columns]), split(tiles[0, c]))

        return carry

    lax.fori_loop(0, couplings, slot, 0)


def beta_call(source, live, place, tiles, buffers, total, half, diag=None):
    count, couplings, size, _ = tiles.shape
    rows, cols = buffers[0].shape[0] // (HALVES if diag is not None else 1), buffers[0].shape[1]
    first = diag is not None
    once = pl.Buffered(buffer_count=1)
    tile_spec = pl.BlockSpec((1, couplings, size, size), lambda j, *_: (j, 0, 0, 0))
    out_spec = pl.BlockSpec((rows, size), lambda j, *_: (half, j))
    if first:
        rows = buffers[0].shape[0]
        out_spec = pl.BlockSpec((rows, size), lambda j, *_: (0, j))
        in_specs = [
            tile_spec,
            pl.BlockSpec((rows, 1), lambda j, *_: (0, 0), pipeline_mode=once),
            pl.BlockSpec((1, cols), lambda j, *_: (0, 0), pipeline_mode=once),
            pl.BlockSpec((rows, cols), lambda j, *_: (0, 0), pipeline_mode=once),
        ]
        operands = (tiles, *diag, *buffers)
        shape = buffers[0].shape
        aliases = {}
    else:
        whole = pl.BlockSpec((rows, cols), lambda j, *_: (0, 0), pipeline_mode=once)
        in_specs = [tile_spec, whole, whole, out_spec]
        operands = (tiles, *buffers, total)
        shape = total.shape
        aliases = {6: 0}
    return pl.pallas_call(
        functools.partial(beta_kernel, couplings, count, first),
        grid_spec=pltpu.PrefetchScalarGridSpec(
            num_scalar_prefetch=3,
            grid=(count,),
            in_specs=in_specs,
            out_specs=out_spec,
        ),
        out_shape=jax.ShapeDtypeStruct(shape, jnp.float32),
        input_output_aliases=aliases,
        compiler_params=pltpu.CompilerParams(vmem_limit_bytes=VMEM_LIMIT),
        cost_estimate=pl.CostEstimate(
            flops=6 * rows * cols * size * couplings // 2,
            bytes_accessed=4 * (tiles.size + 4 * rows * cols),
            transcendentals=0,
        ),
    )(source, live, place, *operands)


def alpha_kernel(couplings, chunk, source, tally, tiles, rows, total, out):
    target, c = pl.program_id(0), pl.program_id(1)

    @pl.when(c == 0)
    def _():
        out[...] = total[...]

    @pl.when(c < tally[target])
    def _():
        tile = split(tiles[0, 0])

        def part(k, carry):
            columns = pl.ds(pl.multiple_of(k * chunk, chunk), chunk)
            out[:, columns] += product(tile, split(rows[:, columns]))
            return carry

        lax.fori_loop(0, out.shape[1] // chunk, part, 0)


def alpha_call(source, tally, tiles, gathered, total):
    count, couplings, size, _ = tiles.shape
    cols = total.shape[1]
    chunk = 256

    def last(i, c, tally):
        return jnp.minimum(c, tally[i] - 1)

    out_spec = pl.BlockSpec((size, cols), lambda i, c, s, t: (i, 0))
    return pl.pallas_call(
        functools.partial(alpha_kernel, couplings, chunk),
        grid_spec=pltpu.PrefetchScalarGridSpec(
            num_scalar_prefetch=2,
            grid=(count, couplings),
            in_specs=[
                pl.BlockSpec((1, 1, size, size), lambda i, c, s, t: (i, last(i, c, t), 0, 0)),
                pl.BlockSpec((size, cols), lambda i, c, s, t: (s[i * couplings + last(i, c, t)], 0)),
                out_spec,
            ],
            out_specs=out_spec,
        ),
        out_shape=jax.ShapeDtypeStruct(total.shape, jnp.float32),
        input_output_aliases={4: 0},
        compiler_params=pltpu.CompilerParams(vmem_limit_bytes=VMEM_LIMIT),
        cost_estimate=pl.CostEstimate(
            flops=6 * total.size * size * couplings // 2,
            bytes_accessed=4 * (tiles.size + total.size * couplings),
            transcendentals=0,
        ),
    )(source, tally, tiles, gathered, total)


def per_device(
    coeffs,
    diag_alpha,
    diag_beta,
    alpha_tiles,
    beta_hamiltonian_tiles,
    alpha_source,
    alpha_live,
    beta_source_block,
    beta_live,
):
    rows = coeffs.shape[0]
    alpha_count = alpha_tiles.shape[0]
    beta_devices = lax.axis_size("beta")
    alpha_index = lax.axis_index("alpha")
    beta_index = lax.axis_index("beta")
    half_rows = rows // HALVES

    rightward = [(j, j + 1) for j in range(beta_devices - 1)]
    leftward = [(j + 1, j) for j in range(beta_devices - 1)]
    pieces = [coeffs[h * half_rows : (h + 1) * half_rows] for h in range(HALVES)]
    arrived = []
    from_left, from_right = list(pieces), list(pieces)
    for _ in range(beta_devices - 1):
        for h in range(HALVES):
            from_left[h] = lax.ppermute(from_left[h], "beta", rightward)
            from_right[h] = lax.ppermute(from_right[h], "beta", leftward)
        arrived.append((list(from_left), list(from_right)))
    gathered = lax.all_gather(coeffs, "alpha", axis=0, tiled=True)

    source = beta_source_block.reshape(-1)
    live = beta_live.reshape(-1)

    def place(step):
        return jnp.stack([beta_index, jnp.full((), step, beta_index.dtype)]).astype(jnp.int32)

    total = beta_call(
        source,
        live,
        place(0),
        beta_hamiltonian_tiles,
        (coeffs,),
        None,
        0,
        (diag_alpha[:, None], diag_beta[None, :]),
    )
    my_source = lax.dynamic_slice_in_dim(alpha_source, alpha_index * alpha_count, alpha_count, 0)
    my_live = lax.dynamic_slice_in_dim(alpha_live, alpha_index * alpha_count, alpha_count, 0)
    for step in range(1, beta_devices):
        if step == beta_devices - 1:
            total = alpha_call(
                my_source.reshape(-1), jnp.sum(my_live, axis=1), alpha_tiles, gathered, total
            )
        lefts, rights = arrived[step - 1]
        for h in range(HALVES):
            total = beta_call(
                source,
                live,
                place(step),
                beta_hamiltonian_tiles,
                (lefts[h], rights[h]),
                total,
                h,
            )
    return total


def solution(mesh):
    return jax.shard_map(
        per_device,
        mesh=mesh,
        in_specs=(
            P("alpha", "beta"),
            P("alpha"),
            P("beta"),
            P("alpha", None, None, None),
            P("beta", None, None, None),
            P(),
            P(),
            P(),
            P(),
        ),
        out_specs=P("alpha", "beta"),
        check_vma=False,
    )
```

```python
import functools

import jax
import jax.numpy as jnp
from jax import lax
from jax.experimental import pallas as pl
from jax.experimental.pallas import tpu as pltpu
from jax.sharding import PartitionSpec as P

HALVES = 2
VMEM_LIMIT = 48 * 1024 * 1024


def split(x):
    high = x.astype(jnp.bfloat16)
    low = (x - high.astype(jnp.float32)).astype(jnp.bfloat16)
    return high, low


def product(a, b):
    a_high, a_low = a
    b_high, b_low = b
    dot = functools.partial(jnp.dot, preferred_element_type=jnp.float32)
    return dot(a_high, b_high) + (dot(a_high, b_low) + dot(a_low, b_high))


def beta_kernel(couplings, count, first, source, live, place, *refs):
    if first:
        tiles, da, db, own, out = refs
        buffers = (own,)
    else:
        tiles, left, right, total, out = refs
        buffers = (left, right)
    size = tiles.shape[-1]
    me, step = place[0], place[1]
    target = pl.program_id(0)
    if first:
        columns = pl.ds(pl.multiple_of(target * size, size), size)
        out[...] = (da[...] + db[:, columns]) * own[:, columns]
    else:
        out[...] = total[...]
    owners = (me,) if first else (me - step, me + step)

    def slot(c, carry):
        at = (me * count + target) * couplings + c
        block = source[at]
        owner = block // count
        inner = block - owner * count
        columns = pl.ds(pl.multiple_of(inner * size, size), size)
        for buffer, wanted in zip(buffers, owners):

            @pl.when(jnp.logical_and(live[at] != 0, owner == wanted))
            def _():
                out[...] += product(split(buffer[:, columns]), split(tiles[0, c]))

        return carry

    lax.fori_loop(0, couplings, slot, 0)


def beta_call(source, live, place, tiles, buffers, total, half, diag=None):
    count, couplings, size, _ = tiles.shape
    rows, cols = buffers[0].shape[0] // (HALVES if diag is not None else 1), buffers[0].shape[1]
    first = diag is not None
    once = pl.Buffered(buffer_count=1)
    tile_spec = pl.BlockSpec((1, couplings, size, size), lambda j, *_: (j, 0, 0, 0))
    out_spec = pl.BlockSpec((rows, size), lambda j, *_: (half, j))
    if first:
        rows = buffers[0].shape[0]
        out_spec = pl.BlockSpec((rows, size), lambda j, *_: (0, j))
        in_specs = [
            tile_spec,
            pl.BlockSpec((rows, 1), lambda j, *_: (0, 0), pipeline_mode=once),
            pl.BlockSpec((1, cols), lambda j, *_: (0, 0), pipeline_mode=once),
            pl.BlockSpec((rows, cols), lambda j, *_: (0, 0), pipeline_mode=once),
        ]
        operands = (tiles, *diag, *buffers)
        shape = buffers[0].shape
        aliases = {}
    else:
        whole = pl.BlockSpec((rows, cols), lambda j, *_: (0, 0), pipeline_mode=once)
        in_specs = [tile_spec, whole, whole, out_spec]
        operands = (tiles, *buffers, total)
        shape = total.shape
        aliases = {6: 0}
    return pl.pallas_call(
        functools.partial(beta_kernel, couplings, count, first),
        grid_spec=pltpu.PrefetchScalarGridSpec(
            num_scalar_prefetch=3,
            grid=(count,),
            in_specs=in_specs,
            out_specs=out_spec,
        ),
        out_shape=jax.ShapeDtypeStruct(shape, jnp.float32),
        input_output_aliases=aliases,
        compiler_params=pltpu.CompilerParams(vmem_limit_bytes=VMEM_LIMIT),
        cost_estimate=pl.CostEstimate(
            flops=6 * rows * cols * size * couplings // 2,
            bytes_accessed=4 * (tiles.size + 4 * rows * cols),
            transcendentals=0,
        ),
    )(source, live, place, *operands)


def alpha_kernel(target, couplings, chunk, source, tally, tiles, rows, total, out):
    c = pl.program_id(0)

    @pl.when(c == 0)
    def _():
        out[...] = total[...]

    @pl.when(c < tally[target])
    def _():
        tile = split(tiles[0, 0])

        def part(k, carry):
            columns = pl.ds(pl.multiple_of(k * chunk, chunk), chunk)
            out[:, columns] += product(tile, split(rows[:, columns]))
            return carry

        lax.fori_loop(0, out.shape[1] // chunk, part, 0)


def alpha_call(target, source, tally, tiles, gathered, total):
    _, couplings, size, _ = tiles.shape
    cols = total.shape[1]
    chunk = 256

    def last(c, tally):
        return jnp.minimum(c, tally[target] - 1)

    out_spec = pl.BlockSpec((size, cols), lambda c, s, t: (target, 0))
    return pl.pallas_call(
        functools.partial(alpha_kernel, target, couplings, chunk),
        grid_spec=pltpu.PrefetchScalarGridSpec(
            num_scalar_prefetch=2,
            grid=(couplings,),
            in_specs=[
                pl.BlockSpec((1, 1, size, size), lambda c, s, t: (target, last(c, t), 0, 0)),
                pl.BlockSpec(
                    (size, cols), lambda c, s, t: (s[target * couplings + last(c, t)], 0)
                ),
                out_spec,
            ],
            out_specs=out_spec,
        ),
        out_shape=jax.ShapeDtypeStruct(total.shape, jnp.float32),
        input_output_aliases={4: 0},
        compiler_params=pltpu.CompilerParams(vmem_limit_bytes=VMEM_LIMIT),
        cost_estimate=pl.CostEstimate(
            flops=6 * size * cols * size * couplings // 2,
            bytes_accessed=4 * size * cols * couplings,
            transcendentals=0,
        ),
    )(source, tally, tiles, gathered, total)


DEVICES = 4
PACKET = 2
PACKETS = 10
SPILL = 4
AHEAD = 4
GROUPS = ((0, 0), (1, 4), (5, 6), (7, 8), (9, 10), (11, 11))


def sizes(blocks):
    others = (DEVICES - 1) * blocks
    flag = 2 * (PACKETS + 1) * SPILL
    spot = flag + 1
    return others, flag, spot, spot + 2 * others


def send_plan_kernel(blocks, couplings, place, source, live, out, need, order, before):
    others, flag, spot, _ = sizes(blocks)
    me = place[0]
    requests = blocks * couplings
    out[flag] = 0
    for way in range(2):
        end = DEVICES - 1 if way == 0 else 0
        last = DEVICES - 2 if way == 0 else 1

        def clear(u, carry):
            need[u] = 0
            order[u] = 0
            out[spot + way * others + u] = 0
            return carry

        lax.fori_loop(0, others, clear, 0)

        def mark(q, carry):
            block = source[end * requests + q]
            owner = block // blocks
            far = end - owner if way == 0 else owner - end

            @pl.when(jnp.logical_and(live[end * requests + q] != 0, far > 0))
            def _():
                need[(far - 1) * blocks + block - owner * blocks] = 1

            return carry

        lax.fori_loop(0, requests, mark, 0)

        def number(u, k):
            before[u] = k

            @pl.when(need[u] != 0)
            def _():
                order[k] = u

            return k + need[u]

        asked = lax.fori_loop(0, others, number, 0)
        before[others] = asked
        sent = jnp.int32(0)
        for p in range(1, PACKETS + 2):
            width = PACKET if p <= PACKETS else SPILL
            ready = before[min(others, blocks + PACKET * max(0, p - 2))]
            after = jnp.minimum(sent + width, ready)
            for s in range(width):
                used = sent + s < after
                u = order[jnp.minimum(sent + s, others - 1)]
                plain = PACKET * (p - 1) + s if p <= 2 * blocks // PACKET else s
                out[(way * (PACKETS + 1) + p - 1) * SPILL + s] = jnp.where(
                    me == last, jnp.where(used, u, s), plain
                )

                @pl.when(used)
                def _():
                    out[spot + way * others + u] = p * SPILL + s

            sent = after
            if p == PACKETS:

                @pl.when(sent < asked)
                def _():
                    out[flag] = 1


def send_plan(place, source, live, blocks, couplings):
    others, _, _, length = sizes(blocks)
    smem = pl.BlockSpec(memory_space=pltpu.SMEM)
    return pl.pallas_call(
        functools.partial(send_plan_kernel, blocks, couplings),
        in_specs=[smem] * 3,
        out_specs=smem,
        out_shape=jax.ShapeDtypeStruct((length,), jnp.int32),
        scratch_shapes=[
            pltpu.SMEM((others,), jnp.int32),
            pltpu.SMEM((others,), jnp.int32),
            pltpu.SMEM((others + 1,), jnp.int32),
        ],
    )(place, source, live)


def work_plan_kernel(blocks, couplings, place, plan, source, live, after, out, packet, buffer):
    others, _, spot, _ = sizes(blocks)
    me = place[0]
    requests = blocks * couplings
    base = len(GROUPS) * (blocks + 1)

    def locate(q, carry):
        block = source[me * requests + q]
        owner = block // blocks
        inner = block - owner * blocks
        way = jnp.where(owner < me, 0, 1)
        far = jnp.abs(owner - me)
        at_end = me == jnp.where(owner < me, DEVICES - 1, 0)
        u = jnp.maximum((far - 1) * blocks + inner, 0)
        ended = plan[spot + way * others + u]
        p = jnp.where(at_end, ended // SPILL, u // PACKET + 1)
        s = jnp.where(at_end, ended % SPILL, u % PACKET)
        own = owner == me
        packet[q] = jnp.where(live[me * requests + q] == 0, -1, jnp.where(own, 0, p))
        buffer[q] = jnp.where(own, inner, way * SPILL + s)
        return carry

    lax.fori_loop(0, requests, locate, 0)
    filled = jnp.int32(0)
    for g, (low, high) in enumerate(GROUPS):

        def target(j, filled):
            out[g * (blocks + 1) + j] = filled

            def slot(c, filled):
                q = j * couplings + c
                p = packet[q]
                mine = jnp.logical_and(p >= low, p <= high)

                @pl.when(mine)
                def _():
                    out[base + filled] = q * 256 + (p - low) * 2 * SPILL + buffer[q]

                return filled + mine.astype(jnp.int32)

            return lax.fori_loop(0, couplings, slot, filled)

        filled = lax.fori_loop(0, blocks, target, filled)
        out[g * (blocks + 1) + blocks] = filled


def work_plan(place, plan, source, live, blocks, couplings, after):
    requests = blocks * couplings
    smem = pl.BlockSpec(memory_space=pltpu.SMEM)
    return pl.pallas_call(
        functools.partial(work_plan_kernel, blocks, couplings),
        in_specs=[smem] * 4 + [pl.BlockSpec(memory_space=pl.ANY)],
        out_specs=smem,
        out_shape=jax.ShapeDtypeStruct(
            (len(GROUPS) * (blocks + 1) + requests,), jnp.int32
        ),
        scratch_shapes=[pltpu.SMEM((requests,), jnp.int32)] * 2,
    )(place, plan, source, live, after)


def pack_kernel(p, blocks, size, held, plan, *refs):
    own = refs[0]
    pool = (refs[1 : 1 + held], refs[1 + held : 1 + 2 * held])
    outs, sems = refs[-3:-1], refs[-1]
    width = outs[0].shape[0]
    for way in range(2):
        for s in range(width):
            u = plan[(way * (PACKETS + 1) + p - 1) * SPILL + s]

            @pl.when(u < blocks)
            def _():
                columns = pl.ds(pl.multiple_of(u * size, size), size)
                pltpu.make_async_copy(
                    own.at[:, columns], outs[way].at[s], sems.at[way, s]
                ).start()

            for r in range(held):

                @pl.when(jnp.logical_and(u >= blocks, (u - blocks) // PACKET == r))
                def _():
                    pltpu.make_async_copy(
                        pool[way][r].at[(u - blocks) % PACKET], outs[way].at[s], sems.at[way, s]
                    ).start()

    for way in range(2):
        for s in range(width):
            pltpu.make_async_copy(
                own.at[:, pl.ds(0, size)], outs[way].at[s], sems.at[way, s]
            ).wait()


def pack(p, plan, coeffs, came, blocks, after):
    held = max(0, min(p - 2, 2 * blocks // PACKET))
    rows, cols = coeffs.shape
    size = cols // blocks
    width = PACKET if p <= PACKETS else SPILL
    any_spec = pl.BlockSpec(memory_space=pl.ANY)
    inputs = [coeffs] + [right for right, _ in came[:held]] + [left for _, left in came[:held]]
    inputs += after
    return pl.pallas_call(
        functools.partial(pack_kernel, p, blocks, size, held),
        grid_spec=pltpu.PrefetchScalarGridSpec(
            num_scalar_prefetch=1,
            grid=(1,),
            in_specs=[any_spec] * len(inputs),
            out_specs=[any_spec] * 2,
            scratch_shapes=[pltpu.SemaphoreType.DMA((2, width))],
        ),
        out_shape=[jax.ShapeDtypeStruct((width, rows, size), jnp.float32)] * 2,
        compiler_params=pltpu.CompilerParams(vmem_limit_bytes=VMEM_LIMIT),
        cost_estimate=pl.CostEstimate(
            flops=0, bytes_accessed=16 * width * rows * size, transcendentals=0
        ),
    )(plan, *inputs)


def work_kernel(g, blocks, couplings, size, held, work, *refs):
    base = len(GROUPS) * (blocks + 1)
    tiles, sources = refs[0], refs[1 : 1 + held]
    out, block_slots, tile_slots, sems = refs[-4:]
    target = pl.program_id(0)
    first, stop = work[g * (blocks + 1)], work[g * (blocks + 1) + blocks]

    def fetch(e):
        slot = e % AHEAD
        entry = work[base + e]
        where = entry % 256
        pltpu.make_async_copy(
            tiles.at[entry // 256], tile_slots.at[slot], sems.at[0, slot]
        ).start()
        if g == 0:
            columns = pl.ds(pl.multiple_of(where * size, size), size)
            pltpu.make_async_copy(
                sources[0].at[:, columns], block_slots.at[slot], sems.at[1, slot]
            ).start()
        else:
            for i in range(held):

                @pl.when(where // SPILL == i)
                def _():
                    pltpu.make_async_copy(
                        sources[i].at[where % SPILL], block_slots.at[slot], sems.at[1, slot]
                    ).start()

    @pl.when(target == 0)
    def _():
        for i in range(AHEAD - 1):

            @pl.when(first + i < stop)
            def _():
                fetch(first + i)

    if g == 0:
        da, db, mine = refs[1 + held : 4 + held]
        out[...] = (da[...] + db[...]) * mine[...]
    else:
        out[...] = refs[1 + held][...]

    def entry(e, carry):
        @pl.when(e + AHEAD - 1 < stop)
        def _():
            fetch(e + AHEAD - 1)

        slot = e % AHEAD
        pltpu.make_async_copy(tiles.at[0], tile_slots.at[slot], sems.at[0, slot]).wait()
        pltpu.make_async_copy(
            block_slots.at[slot], block_slots.at[slot], sems.at[1, slot]
        ).wait()
        tile = split(tile_slots[slot])
        half = out.shape[0] // HALVES
        for h in range(HALVES):
            rows = pl.ds(h * half, half)
            out[rows, :] += product(split(block_slots[slot, rows, :]), tile)
        return carry

    at = g * (blocks + 1) + target
    lax.fori_loop(work[at], work[at + 1], entry, 0)


def work_call(g, work, tiles, sources, rest, after):
    blocks, couplings, size, _ = tiles.shape
    rows, cols = rest[-1].shape
    low, high = GROUPS[g]
    any_spec = pl.BlockSpec(memory_space=pl.ANY)
    column = pl.BlockSpec((rows, size), lambda j, *_: (0, j))
    specs = [column]
    if g == 0:
        specs = [
            pl.BlockSpec((rows, 1), lambda j, *_: (0, 0)),
            pl.BlockSpec((1, size), lambda j, *_: (0, j)),
            column,
        ]
    held = len(sources)
    return pl.pallas_call(
        functools.partial(work_kernel, g, blocks, couplings, size, held),
        grid_spec=pltpu.PrefetchScalarGridSpec(
            num_scalar_prefetch=1,
            grid=(blocks,),
            in_specs=[any_spec] * (1 + held) + specs + [any_spec] * len(after),
            out_specs=column,
            scratch_shapes=[
                pltpu.VMEM((AHEAD, rows, size), jnp.float32),
                pltpu.VMEM((AHEAD, size, size), jnp.float32),
                pltpu.SemaphoreType.DMA((2, AHEAD)),
            ],
        ),
        out_shape=jax.ShapeDtypeStruct((rows, cols), jnp.float32),
        input_output_aliases={} if g == 0 else {2 + held: 0},
        compiler_params=pltpu.CompilerParams(vmem_limit_bytes=VMEM_LIMIT),
        cost_estimate=pl.CostEstimate(
            flops=6 * rows * cols * size * couplings // 8,
            bytes_accessed=8 * rows * cols,
            transcendentals=0,
        ),
    )(work, tiles.reshape(blocks * couplings, size, size), *sources, *rest, *after)


def line_of_four(coeffs, diag, beta_tiles, source, live, me, alpha_steps):
    blocks, couplings, _, _ = beta_tiles.shape
    place = me[None].astype(jnp.int32)
    plan = send_plan(place, source, live, blocks, couplings)
    half = 2 * blocks // PACKET
    came = []

    def send(p, after):
        right, left = pack(p, plan, coeffs, came, blocks, after)
        links = [(j, j + 1) for j in range(DEVICES - 1)]
        links = links[0 if p <= half // 2 else 1 if p <= half else 2 :]
        right_in = lax.ppermute(right, "beta", links)
        left_in = lax.ppermute(
            left, "beta", [(DEVICES - 1 - a, DEVICES - 1 - b) for a, b in links]
        )
        return (right_in, left_in), right

    def group(g):
        low, high = GROUPS[g]
        return [buffer for pair in came[low - 1 : high] for buffer in pair]

    total = None
    for p in range(1, PACKETS + 1):
        arriving, packed = send(p, [] if total is None else [total])
        came.append(arriving)
        if p == 2:
            work = work_plan(place, plan, source, live, blocks, couplings, packed)
            total = work_call(0, work, beta_tiles, [coeffs], [*diag, coeffs], [packed])
        elif p == 6:
            total = work_call(1, work, beta_tiles, group(1), [total], [packed])
        elif p == 8:
            total = work_call(2, work, beta_tiles, group(2), [total], [packed])
        elif p == 9:
            for step in alpha_steps[:1]:
                total = step(total)
    for step in alpha_steps[1:]:
        total = step(total)
    for g in (3, 4):
        total = work_call(g, work, beta_tiles, group(g), [total], [packed])

    def spill(total):
        arriving, _ = send(PACKETS + 1, [])
        return work_call(5, work, beta_tiles, list(arriving), [total], [])

    return lax.cond(plan[sizes(blocks)[1]] != 0, spill, lambda total: total, total)


def per_device(
    coeffs,
    diag_alpha,
    diag_beta,
    alpha_tiles,
    beta_hamiltonian_tiles,
    alpha_source,
    alpha_live,
    beta_source_block,
    beta_live,
):
    rows = coeffs.shape[0]
    alpha_count = alpha_tiles.shape[0]
    beta_devices = lax.axis_size("beta")
    alpha_index = lax.axis_index("alpha")
    beta_index = lax.axis_index("beta")
    half_rows = rows // HALVES
    gathered = lax.all_gather(coeffs, "alpha", axis=0, tiled=True)
    source = beta_source_block.reshape(-1)
    live = beta_live.reshape(-1)
    diag = (diag_alpha[:, None], diag_beta[None, :])
    my_source = lax.dynamic_slice_in_dim(alpha_source, alpha_index * alpha_count, alpha_count, 0)
    my_live = lax.dynamic_slice_in_dim(alpha_live, alpha_index * alpha_count, alpha_count, 0)
    my_source, tally = my_source.reshape(-1), jnp.sum(my_live, axis=1)

    def alpha_step(target):
        return lambda total: alpha_call(target, my_source, tally, alpha_tiles, gathered, total)

    alpha_steps = [alpha_step(target) for target in range(alpha_count)]
    if beta_devices == DEVICES and beta_hamiltonian_tiles.shape[:2] == (8, 8):
        return line_of_four(
            coeffs, diag, beta_hamiltonian_tiles, source, live, beta_index, alpha_steps
        )

    rightward = [(j, j + 1) for j in range(beta_devices - 1)]
    leftward = [(j + 1, j) for j in range(beta_devices - 1)]
    pieces = [coeffs[h * half_rows : (h + 1) * half_rows] for h in range(HALVES)]
    arrived = []
    from_left, from_right = list(pieces), list(pieces)
    for _ in range(beta_devices - 1):
        for h in range(HALVES):
            from_left[h] = lax.ppermute(from_left[h], "beta", rightward)
            from_right[h] = lax.ppermute(from_right[h], "beta", leftward)
        arrived.append((list(from_left), list(from_right)))

    def place(step):
        return jnp.stack([beta_index, jnp.full((), step, beta_index.dtype)]).astype(jnp.int32)

    total = beta_call(
        source,
        live,
        place(0),
        beta_hamiltonian_tiles,
        (coeffs,),
        None,
        0,
        diag,
    )
    for step in range(1, beta_devices):
        if step == beta_devices - 1:
            for alpha in alpha_steps:
                total = alpha(total)
        lefts, rights = arrived[step - 1]
        for h in range(HALVES):
            total = beta_call(
                source,
                live,
                place(step),
                beta_hamiltonian_tiles,
                (lefts[h], rights[h]),
                total,
                h,
            )
    return total


def solution(mesh):
    return jax.shard_map(
        per_device,
        mesh=mesh,
        in_specs=(
            P("alpha", "beta"),
            P("alpha"),
            P("beta"),
            P("alpha", None, None, None),
            P("beta", None, None, None),
            P(),
            P(),
            P(),
            P(),
        ),
        out_specs=P("alpha", "beta"),
        check_vma=False,
    )
```

```python
import functools

import jax
import jax.numpy as jnp
from jax import lax
from jax.experimental import pallas as pl
from jax.experimental.pallas import tpu as pltpu
from jax.sharding import PartitionSpec as P

HALVES = 2
VMEM_LIMIT = 48 * 1024 * 1024


def split(x):
    high = x.astype(jnp.bfloat16)
    low = (x - high.astype(jnp.float32)).astype(jnp.bfloat16)
    return high, low


def product(a, b):
    a_high, a_low = a
    b_high, b_low = b
    dot = functools.partial(jnp.dot, preferred_element_type=jnp.float32)
    return dot(a_high, b_high) + (dot(a_high, b_low) + dot(a_low, b_high))


def beta_kernel(couplings, count, first, source, live, place, *refs):
    if first:
        tiles, da, db, own, out = refs
        buffers = (own,)
    else:
        tiles, left, right, total, out = refs
        buffers = (left, right)
    size = tiles.shape[-1]
    me, step = place[0], place[1]
    target = pl.program_id(0)
    if first:
        columns = pl.ds(pl.multiple_of(target * size, size), size)
        out[...] = (da[...] + db[:, columns]) * own[:, columns]
    else:
        out[...] = total[...]
    owners = (me,) if first else (me - step, me + step)

    def slot(c, carry):
        at = (me * count + target) * couplings + c
        block = source[at]
        owner = block // count
        inner = block - owner * count
        columns = pl.ds(pl.multiple_of(inner * size, size), size)
        for buffer, wanted in zip(buffers, owners):

            @pl.when(jnp.logical_and(live[at] != 0, owner == wanted))
            def _():
                out[...] += product(split(buffer[:, columns]), split(tiles[0, c]))

        return carry

    lax.fori_loop(0, couplings, slot, 0)


def beta_call(source, live, place, tiles, buffers, total, half, diag=None):
    count, couplings, size, _ = tiles.shape
    rows, cols = buffers[0].shape[0] // (HALVES if diag is not None else 1), buffers[0].shape[1]
    first = diag is not None
    once = pl.Buffered(buffer_count=1)
    tile_spec = pl.BlockSpec((1, couplings, size, size), lambda j, *_: (j, 0, 0, 0))
    out_spec = pl.BlockSpec((rows, size), lambda j, *_: (half, j))
    if first:
        rows = buffers[0].shape[0]
        out_spec = pl.BlockSpec((rows, size), lambda j, *_: (0, j))
        in_specs = [
            tile_spec,
            pl.BlockSpec((rows, 1), lambda j, *_: (0, 0), pipeline_mode=once),
            pl.BlockSpec((1, cols), lambda j, *_: (0, 0), pipeline_mode=once),
            pl.BlockSpec((rows, cols), lambda j, *_: (0, 0), pipeline_mode=once),
        ]
        operands = (tiles, *diag, *buffers)
        shape = buffers[0].shape
        aliases = {}
    else:
        whole = pl.BlockSpec((rows, cols), lambda j, *_: (0, 0), pipeline_mode=once)
        in_specs = [tile_spec, whole, whole, out_spec]
        operands = (tiles, *buffers, total)
        shape = total.shape
        aliases = {6: 0}
    return pl.pallas_call(
        functools.partial(beta_kernel, couplings, count, first),
        grid_spec=pltpu.PrefetchScalarGridSpec(
            num_scalar_prefetch=3,
            grid=(count,),
            in_specs=in_specs,
            out_specs=out_spec,
        ),
        out_shape=jax.ShapeDtypeStruct(shape, jnp.float32),
        input_output_aliases=aliases,
        compiler_params=pltpu.CompilerParams(vmem_limit_bytes=VMEM_LIMIT),
        cost_estimate=pl.CostEstimate(
            flops=6 * rows * cols * size * couplings // 2,
            bytes_accessed=4 * (tiles.size + 4 * rows * cols),
            transcendentals=0,
        ),
    )(source, live, place, *operands)


def alpha_kernel(target, couplings, chunk, source, tally, tiles, rows, total, out):
    c = pl.program_id(0)

    @pl.when(c == 0)
    def _():
        out[...] = total[...]

    @pl.when(c < tally[target])
    def _():
        tile = split(tiles[0, 0])

        def part(k, carry):
            columns = pl.ds(pl.multiple_of(k * chunk, chunk), chunk)
            out[:, columns] += product(tile, split(rows[:, columns]))
            return carry

        lax.fori_loop(0, out.shape[1] // chunk, part, 0)


def alpha_call(target, source, tally, tiles, gathered, total):
    _, couplings, size, _ = tiles.shape
    cols = total.shape[1]
    chunk = 256

    def last(c, tally):
        return jnp.minimum(c, tally[target] - 1)

    out_spec = pl.BlockSpec((size, cols), lambda c, s, t: (target, 0))
    return pl.pallas_call(
        functools.partial(alpha_kernel, target, couplings, chunk),
        grid_spec=pltpu.PrefetchScalarGridSpec(
            num_scalar_prefetch=2,
            grid=(couplings,),
            in_specs=[
                pl.BlockSpec((1, 1, size, size), lambda c, s, t: (target, last(c, t), 0, 0)),
                pl.BlockSpec(
                    (size, cols), lambda c, s, t: (s[target * couplings + last(c, t)], 0)
                ),
                out_spec,
            ],
            out_specs=out_spec,
        ),
        out_shape=jax.ShapeDtypeStruct(total.shape, jnp.float32),
        input_output_aliases={4: 0},
        compiler_params=pltpu.CompilerParams(vmem_limit_bytes=VMEM_LIMIT),
        cost_estimate=pl.CostEstimate(
            flops=6 * size * cols * size * couplings // 2,
            bytes_accessed=4 * size * cols * couplings,
            transcendentals=0,
        ),
    )(source, tally, tiles, gathered, total)


DEVICES = 4
PACKET = 2
PACKETS = 10
SPILL = 4
AHEAD = 4
GROUPS = ((0, 0), (1, 4), (5, 6), (7, 8), (9, 10), (11, 11))


def sizes(blocks):
    others = (DEVICES - 1) * blocks
    flag = 2 * (PACKETS + 1) * SPILL
    spot = flag + 1
    return others, flag, spot, spot + 2 * others


def send_plan_kernel(blocks, couplings, place, source, live, out, need, order, before):
    others, flag, spot, _ = sizes(blocks)
    me = place[0]
    requests = blocks * couplings
    out[flag] = 0
    for way in range(2):
        end = DEVICES - 1 if way == 0 else 0
        last = DEVICES - 2 if way == 0 else 1

        def clear(u, carry):
            need[u] = 0
            order[u] = 0
            out[spot + way * others + u] = 0
            return carry

        lax.fori_loop(0, others, clear, 0)

        def mark(q, carry):
            block = source[end * requests + q]
            owner = block // blocks
            far = end - owner if way == 0 else owner - end

            @pl.when(jnp.logical_and(live[end * requests + q] != 0, far > 0))
            def _():
                need[(far - 1) * blocks + block - owner * blocks] = 1

            return carry

        lax.fori_loop(0, requests, mark, 0)

        def number(u, k):
            before[u] = k

            @pl.when(need[u] != 0)
            def _():
                order[k] = u

            return k + need[u]

        asked = lax.fori_loop(0, others, number, 0)
        before[others] = asked
        sent = jnp.int32(0)
        for p in range(1, PACKETS + 2):
            width = PACKET if p <= PACKETS else SPILL
            ready = before[min(others, blocks + PACKET * max(0, p - 2))]
            after = jnp.minimum(sent + width, ready)
            for s in range(width):
                used = sent + s < after
                u = order[jnp.minimum(sent + s, others - 1)]
                plain = PACKET * (p - 1) + s if p <= 2 * blocks // PACKET else s
                out[(way * (PACKETS + 1) + p - 1) * SPILL + s] = jnp.where(
                    me == last, jnp.where(used, u, s), plain
                )

                @pl.when(used)
                def _():
                    out[spot + way * others + u] = p * SPILL + s

            sent = after
            if p == PACKETS:

                @pl.when(sent < asked)
                def _():
                    out[flag] = 1


def send_plan(place, source, live, blocks, couplings):
    others, _, _, length = sizes(blocks)
    smem = pl.BlockSpec(memory_space=pltpu.SMEM)
    return pl.pallas_call(
        functools.partial(send_plan_kernel, blocks, couplings),
        in_specs=[smem] * 3,
        out_specs=smem,
        out_shape=jax.ShapeDtypeStruct((length,), jnp.int32),
        scratch_shapes=[
            pltpu.SMEM((others,), jnp.int32),
            pltpu.SMEM((others,), jnp.int32),
            pltpu.SMEM((others + 1,), jnp.int32),
        ],
    )(place, source, live)


def work_plan_kernel(blocks, couplings, place, plan, source, live, after, out, packet, buffer):
    others, _, spot, _ = sizes(blocks)
    me = place[0]
    requests = blocks * couplings
    base = len(GROUPS) * (blocks + 1)

    def locate(q, carry):
        block = source[me * requests + q]
        owner = block // blocks
        inner = block - owner * blocks
        way = jnp.where(owner < me, 0, 1)
        far = jnp.abs(owner - me)
        at_end = me == jnp.where(owner < me, DEVICES - 1, 0)
        u = jnp.maximum((far - 1) * blocks + inner, 0)
        ended = plan[spot + way * others + u]
        p = jnp.where(at_end, ended // SPILL, u // PACKET + 1)
        s = jnp.where(at_end, ended % SPILL, u % PACKET)
        own = owner == me
        packet[q] = jnp.where(live[me * requests + q] == 0, -1, jnp.where(own, 0, p))
        buffer[q] = jnp.where(own, inner, way * SPILL + s)
        return carry

    lax.fori_loop(0, requests, locate, 0)
    filled = jnp.int32(0)
    for g, (low, high) in enumerate(GROUPS):

        def target(j, filled):
            out[g * (blocks + 1) + j] = filled

            def slot(c, filled):
                q = j * couplings + c
                p = packet[q]
                mine = jnp.logical_and(p >= low, p <= high)

                @pl.when(mine)
                def _():
                    out[base + filled] = q * 256 + (p - low) * 2 * SPILL + buffer[q]

                return filled + mine.astype(jnp.int32)

            return lax.fori_loop(0, couplings, slot, filled)

        filled = lax.fori_loop(0, blocks, target, filled)
        out[g * (blocks + 1) + blocks] = filled


def work_plan(place, plan, source, live, blocks, couplings, after):
    requests = blocks * couplings
    smem = pl.BlockSpec(memory_space=pltpu.SMEM)
    return pl.pallas_call(
        functools.partial(work_plan_kernel, blocks, couplings),
        in_specs=[smem] * 4 + [pl.BlockSpec(memory_space=pl.ANY)],
        out_specs=smem,
        out_shape=jax.ShapeDtypeStruct(
            (len(GROUPS) * (blocks + 1) + requests,), jnp.int32
        ),
        scratch_shapes=[pltpu.SMEM((requests,), jnp.int32)] * 2,
    )(place, plan, source, live, after)


def pack_kernel(p, blocks, size, held, plan, *refs):
    own = refs[0]
    pool = (refs[1 : 1 + held], refs[1 + held : 1 + 2 * held])
    outs, sems = refs[-3:-1], refs[-1]
    width = outs[0].shape[0]
    for way in range(2):
        for s in range(width):
            u = plan[(way * (PACKETS + 1) + p - 1) * SPILL + s]

            @pl.when(u < blocks)
            def _():
                columns = pl.ds(pl.multiple_of(u * size, size), size)
                pltpu.make_async_copy(
                    own.at[:, columns], outs[way].at[s], sems.at[way, s]
                ).start()

            for r in range(held):

                @pl.when(jnp.logical_and(u >= blocks, (u - blocks) // PACKET == r))
                def _():
                    pltpu.make_async_copy(
                        pool[way][r].at[(u - blocks) % PACKET], outs[way].at[s], sems.at[way, s]
                    ).start()

    for way in range(2):
        for s in range(width):
            pltpu.make_async_copy(
                outs[way].at[s], outs[way].at[s], sems.at[way, s]
            ).wait()


def pack(p, plan, coeffs, came, blocks, after):
    held = max(0, min(p - 2, 2 * blocks // PACKET))
    rows, cols = coeffs.shape
    size = cols // blocks
    width = PACKET if p <= PACKETS else SPILL
    any_spec = pl.BlockSpec(memory_space=pl.ANY)
    inputs = [coeffs] + [right for right, _ in came[:held]] + [left for _, left in came[:held]]
    inputs += after
    return pl.pallas_call(
        functools.partial(pack_kernel, p, blocks, size, held),
        grid_spec=pltpu.PrefetchScalarGridSpec(
            num_scalar_prefetch=1,
            grid=(1,),
            in_specs=[any_spec] * len(inputs),
            out_specs=[pl.BlockSpec((width, rows, size), lambda i, *_: (0, 0, 0))] * 2,
            scratch_shapes=[pltpu.SemaphoreType.DMA((2, width))],
        ),
        out_shape=[jax.ShapeDtypeStruct((width, rows, size), jnp.float32)] * 2,
        compiler_params=pltpu.CompilerParams(vmem_limit_bytes=VMEM_LIMIT),
        cost_estimate=pl.CostEstimate(
            flops=0, bytes_accessed=16 * width * rows * size, transcendentals=0
        ),
    )(plan, *inputs)


def work_kernel(g, blocks, couplings, size, held, work, *refs):
    base = len(GROUPS) * (blocks + 1)
    tiles, sources = refs[0], refs[1 : 1 + held]
    out, block_slots, tile_slots, sems = refs[-4:]
    target = pl.program_id(0)
    first, stop = work[g * (blocks + 1)], work[g * (blocks + 1) + blocks]

    def fetch(e):
        slot = e % AHEAD
        entry = work[base + e]
        where = entry % 256
        pltpu.make_async_copy(
            tiles.at[entry // 256], tile_slots.at[slot], sems.at[0, slot]
        ).start()
        if g == 0:
            columns = pl.ds(pl.multiple_of(where * size, size), size)
            pltpu.make_async_copy(
                sources[0].at[:, columns], block_slots.at[slot], sems.at[1, slot]
            ).start()
        else:
            for i in range(held):

                @pl.when(where // SPILL == i)
                def _():
                    pltpu.make_async_copy(
                        sources[i].at[where % SPILL], block_slots.at[slot], sems.at[1, slot]
                    ).start()

    @pl.when(target == 0)
    def _():
        for i in range(AHEAD - 1):

            @pl.when(first + i < stop)
            def _():
                fetch(first + i)

    if g == 0:
        da, db, mine = refs[1 + held : 4 + held]
        out[...] = (da[...] + db[...]) * mine[...]
    else:
        out[...] = refs[1 + held][...]

    def entry(e, carry):
        @pl.when(e + AHEAD - 1 < stop)
        def _():
            fetch(e + AHEAD - 1)

        slot = e % AHEAD
        pltpu.make_async_copy(tiles.at[0], tile_slots.at[slot], sems.at[0, slot]).wait()
        pltpu.make_async_copy(
            block_slots.at[slot], block_slots.at[slot], sems.at[1, slot]
        ).wait()
        tile = split(tile_slots[slot])
        half = out.shape[0] // HALVES
        for h in range(HALVES):
            rows = pl.ds(h * half, half)
            out[rows, :] += product(split(block_slots[slot, rows, :]), tile)
        return carry

    at = g * (blocks + 1) + target
    lax.fori_loop(work[at], work[at + 1], entry, 0)


def work_call(g, work, tiles, sources, rest, after):
    blocks, couplings, size, _ = tiles.shape
    rows, cols = rest[-1].shape
    low, high = GROUPS[g]
    any_spec = pl.BlockSpec(memory_space=pl.ANY)
    column = pl.BlockSpec((rows, size), lambda j, *_: (0, j))
    specs = [column]
    if g == 0:
        specs = [
            pl.BlockSpec((rows, 1), lambda j, *_: (0, 0)),
            pl.BlockSpec((1, size), lambda j, *_: (0, j)),
            column,
        ]
    held = len(sources)
    return pl.pallas_call(
        functools.partial(work_kernel, g, blocks, couplings, size, held),
        grid_spec=pltpu.PrefetchScalarGridSpec(
            num_scalar_prefetch=1,
            grid=(blocks,),
            in_specs=[any_spec] * (1 + held) + specs + [any_spec] * len(after),
            out_specs=column,
            scratch_shapes=[
                pltpu.VMEM((AHEAD, rows, size), jnp.float32),
                pltpu.VMEM((AHEAD, size, size), jnp.float32),
                pltpu.SemaphoreType.DMA((2, AHEAD)),
            ],
        ),
        out_shape=jax.ShapeDtypeStruct((rows, cols), jnp.float32),
        input_output_aliases={} if g == 0 else {2 + held: 0},
        compiler_params=pltpu.CompilerParams(vmem_limit_bytes=VMEM_LIMIT),
        cost_estimate=pl.CostEstimate(
            flops=6 * rows * cols * size * couplings // 8,
            bytes_accessed=8 * rows * cols,
            transcendentals=0,
        ),
    )(work, tiles.reshape(blocks * couplings, size, size), *sources, *rest, *after)


def line_of_four(coeffs, diag, beta_tiles, source, live, me, alpha_steps):
    blocks, couplings, _, _ = beta_tiles.shape
    place = me[None].astype(jnp.int32)
    plan = send_plan(place, source, live, blocks, couplings)
    half = 2 * blocks // PACKET
    came = []

    def send(p, after):
        right, left = pack(p, plan, coeffs, came, blocks, after)
        links = [(j, j + 1) for j in range(DEVICES - 1)]
        links = links[0 if p <= half // 2 else 1 if p <= half else 2 :]
        right_in = lax.ppermute(right, "beta", links)
        left_in = lax.ppermute(
            left, "beta", [(DEVICES - 1 - a, DEVICES - 1 - b) for a, b in links]
        )
        return (right_in, left_in), right

    def group(g):
        low, high = GROUPS[g]
        return [buffer for pair in came[low - 1 : high] for buffer in pair]

    total = None
    for p in range(1, PACKETS + 1):
        arriving, packed = send(p, [] if total is None else [total])
        came.append(arriving)
        if p == 2:
            work = work_plan(place, plan, source, live, blocks, couplings, packed)
            total = work_call(0, work, beta_tiles, [coeffs], [*diag, coeffs], [packed])
        elif p == 6:
            total = work_call(1, work, beta_tiles, group(1), [total], [packed])
        elif p == 8:
            total = work_call(2, work, beta_tiles, group(2), [total], [packed])
        elif p == 9:
            for step in alpha_steps[:1]:
                total = step(total)
    for step in alpha_steps[1:]:
        total = step(total)
    total = work_call(3, work, beta_tiles, group(3), [total], [packed])

    def spill(total):
        arriving, _ = send(PACKETS + 1, [])
        return work_call(5, work, beta_tiles, list(arriving), [total], [])

    total = lax.cond(plan[sizes(blocks)[1]] != 0, spill, lambda total: total, total)
    return work_call(4, work, beta_tiles, group(4), [total], [])


def per_device(
    coeffs,
    diag_alpha,
    diag_beta,
    alpha_tiles,
    beta_hamiltonian_tiles,
    alpha_source,
    alpha_live,
    beta_source_block,
    beta_live,
):
    rows = coeffs.shape[0]
    alpha_count = alpha_tiles.shape[0]
    beta_devices = lax.axis_size("beta")
    alpha_index = lax.axis_index("alpha")
    beta_index = lax.axis_index("beta")
    half_rows = rows // HALVES
    gathered = lax.all_gather(coeffs, "alpha", axis=0, tiled=True)
    source = beta_source_block.reshape(-1)
    live = beta_live.reshape(-1)
    diag = (diag_alpha[:, None], diag_beta[None, :])
    my_source = lax.dynamic_slice_in_dim(alpha_source, alpha_index * alpha_count, alpha_count, 0)
    my_live = lax.dynamic_slice_in_dim(alpha_live, alpha_index * alpha_count, alpha_count, 0)
    my_source, tally = my_source.reshape(-1), jnp.sum(my_live, axis=1)

    def alpha_step(target):
        return lambda total: alpha_call(target, my_source, tally, alpha_tiles, gathered, total)

    alpha_steps = [alpha_step(target) for target in range(alpha_count)]
    if beta_devices == DEVICES and beta_hamiltonian_tiles.shape[:2] == (8, 8):
        return line_of_four(
            coeffs, diag, beta_hamiltonian_tiles, source, live, beta_index, alpha_steps
        )

    rightward = [(j, j + 1) for j in range(beta_devices - 1)]
    leftward = [(j + 1, j) for j in range(beta_devices - 1)]
    pieces = [coeffs[h * half_rows : (h + 1) * half_rows] for h in range(HALVES)]
    arrived = []
    from_left, from_right = list(pieces), list(pieces)
    for _ in range(beta_devices - 1):
        for h in range(HALVES):
            from_left[h] = lax.ppermute(from_left[h], "beta", rightward)
            from_right[h] = lax.ppermute(from_right[h], "beta", leftward)
        arrived.append((list(from_left), list(from_right)))

    def place(step):
        return jnp.stack([beta_index, jnp.full((), step, beta_index.dtype)]).astype(jnp.int32)

    total = beta_call(
        source,
        live,
        place(0),
        beta_hamiltonian_tiles,
        (coeffs,),
        None,
        0,
        diag,
    )
    for step in range(1, beta_devices):
        if step == beta_devices - 1:
            for alpha in alpha_steps:
                total = alpha(total)
        lefts, rights = arrived[step - 1]
        for h in range(HALVES):
            total = beta_call(
                source,
                live,
                place(step),
                beta_hamiltonian_tiles,
                (lefts[h], rights[h]),
                total,
                h,
            )
    return total


def solution(mesh):
    return jax.shard_map(
        per_device,
        mesh=mesh,
        in_specs=(
            P("alpha", "beta"),
            P("alpha"),
            P("beta"),
            P("alpha", None, None, None),
            P("beta", None, None, None),
            P(),
            P(),
            P(),
            P(),
        ),
        out_specs=P("alpha", "beta"),
        check_vma=False,
    )
```

```python
import functools

import jax
import jax.numpy as jnp
from jax import lax
from jax.experimental import pallas as pl
from jax.experimental.pallas import tpu as pltpu
from jax.sharding import PartitionSpec as P

HALVES = 2
VMEM_LIMIT = 48 * 1024 * 1024


def split(x):
    high = x.astype(jnp.bfloat16)
    low = (x - high.astype(jnp.float32)).astype(jnp.bfloat16)
    return high, low


def product(a, b):
    a_high, a_low = a
    b_high, b_low = b
    dot = functools.partial(jnp.dot, preferred_element_type=jnp.float32)
    return dot(a_high, b_high) + (dot(a_high, b_low) + dot(a_low, b_high))


def beta_kernel(couplings, count, first, source, live, place, *refs):
    if first:
        tiles, da, db, own, out = refs
        buffers = (own,)
    else:
        tiles, left, right, total, out = refs
        buffers = (left, right)
    size = tiles.shape[-1]
    me, step = place[0], place[1]
    target = pl.program_id(0)
    if first:
        columns = pl.ds(pl.multiple_of(target * size, size), size)
        out[...] = (da[...] + db[:, columns]) * own[:, columns]
    else:
        out[...] = total[...]
    owners = (me,) if first else (me - step, me + step)

    def slot(c, carry):
        at = (me * count + target) * couplings + c
        block = source[at]
        owner = block // count
        inner = block - owner * count
        columns = pl.ds(pl.multiple_of(inner * size, size), size)
        for buffer, wanted in zip(buffers, owners):

            @pl.when(jnp.logical_and(live[at] != 0, owner == wanted))
            def _():
                out[...] += product(split(buffer[:, columns]), split(tiles[0, c]))

        return carry

    lax.fori_loop(0, couplings, slot, 0)


def beta_call(source, live, place, tiles, buffers, total, half, diag=None):
    count, couplings, size, _ = tiles.shape
    rows, cols = buffers[0].shape[0] // (HALVES if diag is not None else 1), buffers[0].shape[1]
    first = diag is not None
    once = pl.Buffered(buffer_count=1)
    tile_spec = pl.BlockSpec((1, couplings, size, size), lambda j, *_: (j, 0, 0, 0))
    out_spec = pl.BlockSpec((rows, size), lambda j, *_: (half, j))
    if first:
        rows = buffers[0].shape[0]
        out_spec = pl.BlockSpec((rows, size), lambda j, *_: (0, j))
        in_specs = [
            tile_spec,
            pl.BlockSpec((rows, 1), lambda j, *_: (0, 0), pipeline_mode=once),
            pl.BlockSpec((1, cols), lambda j, *_: (0, 0), pipeline_mode=once),
            pl.BlockSpec((rows, cols), lambda j, *_: (0, 0), pipeline_mode=once),
        ]
        operands = (tiles, *diag, *buffers)
        shape = buffers[0].shape
        aliases = {}
    else:
        whole = pl.BlockSpec((rows, cols), lambda j, *_: (0, 0), pipeline_mode=once)
        in_specs = [tile_spec, whole, whole, out_spec]
        operands = (tiles, *buffers, total)
        shape = total.shape
        aliases = {6: 0}
    return pl.pallas_call(
        functools.partial(beta_kernel, couplings, count, first),
        grid_spec=pltpu.PrefetchScalarGridSpec(
            num_scalar_prefetch=3,
            grid=(count,),
            in_specs=in_specs,
            out_specs=out_spec,
        ),
        out_shape=jax.ShapeDtypeStruct(shape, jnp.float32),
        input_output_aliases=aliases,
        compiler_params=pltpu.CompilerParams(vmem_limit_bytes=VMEM_LIMIT),
        cost_estimate=pl.CostEstimate(
            flops=6 * rows * cols * size * couplings // 2,
            bytes_accessed=4 * (tiles.size + 4 * rows * cols),
            transcendentals=0,
        ),
    )(source, live, place, *operands)


def alpha_kernel(target, couplings, chunk, source, tally, tiles, rows, total, out):
    c = pl.program_id(0)

    @pl.when(c == 0)
    def _():
        out[...] = total[...]

    @pl.when(c < tally[target])
    def _():
        tile = split(tiles[0, 0])

        def part(k, carry):
            columns = pl.ds(pl.multiple_of(k * chunk, chunk), chunk)
            out[:, columns] += product(tile, split(rows[:, columns]))
            return carry

        lax.fori_loop(0, out.shape[1] // chunk, part, 0)


def alpha_call(target, source, tally, tiles, gathered, total):
    _, couplings, size, _ = tiles.shape
    cols = total.shape[1]
    chunk = 256

    def last(c, tally):
        return jnp.minimum(c, tally[target] - 1)

    out_spec = pl.BlockSpec((size, cols), lambda c, s, t: (target, 0))
    return pl.pallas_call(
        functools.partial(alpha_kernel, target, couplings, chunk),
        grid_spec=pltpu.PrefetchScalarGridSpec(
            num_scalar_prefetch=2,
            grid=(couplings,),
            in_specs=[
                pl.BlockSpec((1, 1, size, size), lambda c, s, t: (target, last(c, t), 0, 0)),
                pl.BlockSpec(
                    (size, cols), lambda c, s, t: (s[target * couplings + last(c, t)], 0)
                ),
                out_spec,
            ],
            out_specs=out_spec,
        ),
        out_shape=jax.ShapeDtypeStruct(total.shape, jnp.float32),
        input_output_aliases={4: 0},
        compiler_params=pltpu.CompilerParams(vmem_limit_bytes=VMEM_LIMIT),
        cost_estimate=pl.CostEstimate(
            flops=6 * size * cols * size * couplings // 2,
            bytes_accessed=4 * size * cols * couplings,
            transcendentals=0,
        ),
    )(source, tally, tiles, gathered, total)


DEVICES = 4
PACKET = 2
PACKETS = 12
FORMS = (9, 10, 12)
AHEAD = 4
GROUPS = ((0, 0), (1, 4), (5, 6), (7, 8), (9, 10), (11, 12))


def sizes(blocks):
    others = (DEVICES - 1) * blocks
    flag = 2 * PACKETS * PACKET
    spot = flag + 1
    return others, flag, spot, spot + 2 * others


def send_plan_kernel(blocks, couplings, place, source, live, out, need, order, before):
    others, flag, spot, _ = sizes(blocks)
    me = place[0]
    requests = blocks * couplings
    counts = []
    for way in range(2):
        end = DEVICES - 1 if way == 0 else 0
        base = way * others
        base_before = way * (others + 1)

        def clear(u, carry):
            need[base + u] = 0
            order[base + u] = 0
            out[spot + base + u] = 0
            return carry

        lax.fori_loop(0, others, clear, 0)

        def mark(q, carry):
            block = source[end * requests + q]
            owner = block // blocks
            far = end - owner if way == 0 else owner - end

            @pl.when(jnp.logical_and(live[end * requests + q] != 0, far > 0))
            def _():
                need[base + (far - 1) * blocks + block - owner * blocks] = 1

            return carry

        lax.fori_loop(0, requests, mark, 0)

        def number(u, k):
            before[base_before + u] = k

            @pl.when(need[base + u] != 0)
            def _():
                order[base + k] = u

            return k + need[base + u]

        asked = lax.fori_loop(0, others, number, 0)
        before[base_before + others] = asked
        counts.append(asked)
    most = jnp.maximum(*counts)
    form = (most > FORMS[0] * PACKET).astype(jnp.int32) + (most > FORMS[1] * PACKET).astype(
        jnp.int32
    )
    out[flag] = form
    for way in range(2):
        last = DEVICES - 2 if way == 0 else 1
        base = way * others
        base_before = way * (others + 1)
        sent = jnp.int32(0)
        for p in range(1, PACKETS + 1):
            slow = before[base_before + min(others, blocks + PACKET * max(0, p - 2))]
            fast = before[base_before + min(others, blocks + PACKET * (p - 1 if p > 2 else 0))]
            ready = jnp.where(form == 0, fast, slow)
            after = jnp.minimum(sent + PACKET, ready)
            for s in range(PACKET):
                used = sent + s < after
                u = order[base + jnp.minimum(sent + s, others - 1)]
                plain = PACKET * (p - 1) + s if p <= 2 * blocks // PACKET else s
                out[(way * PACKETS + p - 1) * PACKET + s] = jnp.where(
                    me == last, jnp.where(used, u, s), plain
                )

                @pl.when(used)
                def _():
                    out[spot + base + u] = p * PACKET + s

            sent = after


def send_plan(place, source, live, blocks, couplings):
    others, _, _, length = sizes(blocks)
    smem = pl.BlockSpec(memory_space=pltpu.SMEM)
    return pl.pallas_call(
        functools.partial(send_plan_kernel, blocks, couplings),
        in_specs=[smem] * 3,
        out_specs=smem,
        out_shape=jax.ShapeDtypeStruct((length,), jnp.int32),
        scratch_shapes=[
            pltpu.SMEM((2 * others,), jnp.int32),
            pltpu.SMEM((2 * others,), jnp.int32),
            pltpu.SMEM((2 * (others + 1),), jnp.int32),
        ],
    )(place, source, live)


def work_plan_kernel(blocks, couplings, place, plan, source, live, after, out, packet, buffer):
    others, _, spot, _ = sizes(blocks)
    me = place[0]
    requests = blocks * couplings
    base = len(GROUPS) * (blocks + 1)

    def locate(q, carry):
        block = source[me * requests + q]
        owner = block // blocks
        inner = block - owner * blocks
        way = jnp.where(owner < me, 0, 1)
        far = jnp.abs(owner - me)
        at_end = me == jnp.where(owner < me, DEVICES - 1, 0)
        u = jnp.maximum((far - 1) * blocks + inner, 0)
        ended = plan[spot + way * others + u]
        p = jnp.where(at_end, ended // PACKET, u // PACKET + 1)
        s = jnp.where(at_end, ended % PACKET, u % PACKET)
        own = owner == me
        packet[q] = jnp.where(live[me * requests + q] == 0, -1, jnp.where(own, 0, p))
        buffer[q] = jnp.where(own, inner, way * PACKET + s)
        return carry

    lax.fori_loop(0, requests, locate, 0)
    filled = jnp.int32(0)
    for g, (low, high) in enumerate(GROUPS):

        def target(j, filled):
            out[g * (blocks + 1) + j] = filled

            def slot(c, filled):
                q = j * couplings + c
                p = packet[q]
                mine = jnp.logical_and(p >= low, p <= high)

                @pl.when(mine)
                def _():
                    out[base + filled] = q * 256 + (p - low) * 2 * PACKET + buffer[q]

                return filled + mine.astype(jnp.int32)

            return lax.fori_loop(0, couplings, slot, filled)

        filled = lax.fori_loop(0, blocks, target, filled)
        out[g * (blocks + 1) + blocks] = filled


def work_plan(place, plan, source, live, blocks, couplings, after):
    requests = blocks * couplings
    smem = pl.BlockSpec(memory_space=pltpu.SMEM)
    return pl.pallas_call(
        functools.partial(work_plan_kernel, blocks, couplings),
        in_specs=[smem] * 4 + [pl.BlockSpec(memory_space=pl.ANY)],
        out_specs=smem,
        out_shape=jax.ShapeDtypeStruct(
            (len(GROUPS) * (blocks + 1) + requests,), jnp.int32
        ),
        scratch_shapes=[pltpu.SMEM((requests,), jnp.int32)] * 2,
    )(place, plan, source, live, after)


def pack_kernel(p, blocks, size, held, plan, *refs):
    own = refs[0]
    pool = (refs[1 : 1 + held], refs[1 + held : 1 + 2 * held])
    outs, sems = refs[-3:-1], refs[-1]
    width = outs[0].shape[0]
    for way in range(2):
        for s in range(width):
            u = plan[(way * PACKETS + p - 1) * PACKET + s]

            @pl.when(u < blocks)
            def _():
                columns = pl.ds(pl.multiple_of(u * size, size), size)
                pltpu.make_async_copy(
                    own.at[:, columns], outs[way].at[s], sems.at[way, s]
                ).start()

            for r in range(held):

                @pl.when(jnp.logical_and(u >= blocks, (u - blocks) // PACKET == r))
                def _():
                    pltpu.make_async_copy(
                        pool[way][r].at[(u - blocks) % PACKET], outs[way].at[s], sems.at[way, s]
                    ).start()

    for way in range(2):
        for s in range(width):
            pltpu.make_async_copy(
                outs[way].at[s], outs[way].at[s], sems.at[way, s]
            ).wait()


def pack(p, lag, plan, coeffs, came, blocks, after):
    held = 0 if p <= 2 else min(p - lag, 2 * blocks // PACKET)
    rows, cols = coeffs.shape
    size = cols // blocks
    width = PACKET
    any_spec = pl.BlockSpec(memory_space=pl.ANY)
    inputs = [coeffs] + [right for right, _ in came[:held]] + [left for _, left in came[:held]]
    inputs += after
    return pl.pallas_call(
        functools.partial(pack_kernel, p, blocks, size, held),
        grid_spec=pltpu.PrefetchScalarGridSpec(
            num_scalar_prefetch=1,
            grid=(1,),
            in_specs=[any_spec] * len(inputs),
            out_specs=[pl.BlockSpec((width, rows, size), lambda i, *_: (0, 0, 0))] * 2,
            scratch_shapes=[pltpu.SemaphoreType.DMA((2, width))],
        ),
        out_shape=[jax.ShapeDtypeStruct((width, rows, size), jnp.float32)] * 2,
        compiler_params=pltpu.CompilerParams(vmem_limit_bytes=VMEM_LIMIT),
        cost_estimate=pl.CostEstimate(
            flops=0, bytes_accessed=16 * width * rows * size, transcendentals=0
        ),
    )(plan, *inputs)


def work_kernel(g, blocks, couplings, size, held, work, *refs):
    base = len(GROUPS) * (blocks + 1)
    tiles, sources = refs[0], refs[1 : 1 + held]
    out, block_slots, tile_slots, sems = refs[-4:]
    target = pl.program_id(0)
    first, stop = work[g * (blocks + 1)], work[g * (blocks + 1) + blocks]

    def fetch(e):
        slot = e % AHEAD
        entry = work[base + e]
        where = entry % 256
        pltpu.make_async_copy(
            tiles.at[entry // 256], tile_slots.at[slot], sems.at[0, slot]
        ).start()
        if g == 0:
            columns = pl.ds(pl.multiple_of(where * size, size), size)
            pltpu.make_async_copy(
                sources[0].at[:, columns], block_slots.at[slot], sems.at[1, slot]
            ).start()
        else:
            for i in range(held):

                @pl.when(where // PACKET == i)
                def _():
                    pltpu.make_async_copy(
                        sources[i].at[where % PACKET], block_slots.at[slot], sems.at[1, slot]
                    ).start()

    @pl.when(target == 0)
    def _():
        for i in range(AHEAD - 1):

            @pl.when(first + i < stop)
            def _():
                fetch(first + i)

    if g == 0:
        da, db, mine = refs[1 + held : 4 + held]
        out[...] = (da[...] + db[...]) * mine[...]
    else:
        out[...] = refs[1 + held][...]

    def entry(e, carry):
        @pl.when(e + AHEAD - 1 < stop)
        def _():
            fetch(e + AHEAD - 1)

        slot = e % AHEAD
        pltpu.make_async_copy(tiles.at[0], tile_slots.at[slot], sems.at[0, slot]).wait()
        pltpu.make_async_copy(
            block_slots.at[slot], block_slots.at[slot], sems.at[1, slot]
        ).wait()
        tile = split(tile_slots[slot])
        half = out.shape[0] // HALVES
        for h in range(HALVES):
            rows = pl.ds(h * half, half)
            out[rows, :] += product(split(block_slots[slot, rows, :]), tile)
        return carry

    at = g * (blocks + 1) + target
    lax.fori_loop(work[at], work[at + 1], entry, 0)


def work_call(g, work, tiles, sources, rest, after):
    blocks, couplings, size, _ = tiles.shape
    rows, cols = rest[-1].shape
    low, high = GROUPS[g]
    any_spec = pl.BlockSpec(memory_space=pl.ANY)
    column = pl.BlockSpec((rows, size), lambda j, *_: (0, j))
    specs = [column]
    if g == 0:
        specs = [
            pl.BlockSpec((rows, 1), lambda j, *_: (0, 0)),
            pl.BlockSpec((1, size), lambda j, *_: (0, j)),
            column,
        ]
    held = len(sources)
    return pl.pallas_call(
        functools.partial(work_kernel, g, blocks, couplings, size, held),
        grid_spec=pltpu.PrefetchScalarGridSpec(
            num_scalar_prefetch=1,
            grid=(blocks,),
            in_specs=[any_spec] * (1 + held) + specs + [any_spec] * len(after),
            out_specs=column,
            scratch_shapes=[
                pltpu.VMEM((AHEAD, rows, size), jnp.float32),
                pltpu.VMEM((AHEAD, size, size), jnp.float32),
                pltpu.SemaphoreType.DMA((2, AHEAD)),
            ],
        ),
        out_shape=jax.ShapeDtypeStruct((rows, cols), jnp.float32),
        input_output_aliases={} if g == 0 else {2 + held: 0},
        compiler_params=pltpu.CompilerParams(vmem_limit_bytes=VMEM_LIMIT),
        cost_estimate=pl.CostEstimate(
            flops=6 * rows * cols * size * couplings // 8,
            bytes_accessed=8 * rows * cols,
            transcendentals=0,
        ),
    )(work, tiles.reshape(blocks * couplings, size, size), *sources, *rest, *after)


def line_of_four(form, plan, place, coeffs, diag, beta_tiles, source, live, alpha_steps):
    blocks, couplings, _, _ = beta_tiles.shape
    packets = FORMS[form]
    lag = 1 if form == 0 else 2
    half = 2 * blocks // PACKET
    came = []

    def send(p, after):
        right, left = pack(p, lag, plan, coeffs, came, blocks, after)
        links = [(j, j + 1) for j in range(DEVICES - 1)]
        links = links[0 if p <= half // 2 else 1 if p <= half else 2 :]
        right_in = lax.ppermute(right, "beta", links)
        left_in = lax.ppermute(
            left, "beta", [(DEVICES - 1 - a, DEVICES - 1 - b) for a, b in links]
        )
        return (right_in, left_in), right

    def add(g, total, packed):
        low, high = GROUPS[g]
        buffers = [buffer for pair in came[low - 1 : high] for buffer in pair]
        return work_call(g, work, beta_tiles, buffers, [total], [packed])

    total = None
    for p in range(1, packets + 1):
        arriving, packed = send(p, [] if total is None else [total])
        came.append(arriving)
        if p == 2:
            work = work_plan(place, plan, source, live, blocks, couplings, packed)
            total = work_call(0, work, beta_tiles, [coeffs], [*diag, coeffs], [packed])
        elif p == 4 + lag:
            total = add(1, total, packed)
        elif p == 6 + lag:
            total = add(2, total, packed)
        elif p == 7 + lag:
            total = alpha_steps[0](total)
        elif p == 10 and packets > 10:
            for step in alpha_steps[1:]:
                total = step(total)
            total = add(3, total, packed)
    if packets <= 10:
        for step in alpha_steps[1:]:
            total = step(total)
        total = add(3, total, packed)
    total = add(4, total, packed)
    return add(5, total, packed) if packets > 10 else total


def per_device(
    coeffs,
    diag_alpha,
    diag_beta,
    alpha_tiles,
    beta_hamiltonian_tiles,
    alpha_source,
    alpha_live,
    beta_source_block,
    beta_live,
):
    rows = coeffs.shape[0]
    alpha_count = alpha_tiles.shape[0]
    beta_devices = lax.axis_size("beta")
    alpha_index = lax.axis_index("alpha")
    beta_index = lax.axis_index("beta")
    half_rows = rows // HALVES
    source = beta_source_block.reshape(-1)
    live = beta_live.reshape(-1)
    diag = (diag_alpha[:, None], diag_beta[None, :])
    my_source = lax.dynamic_slice_in_dim(alpha_source, alpha_index * alpha_count, alpha_count, 0)
    my_live = lax.dynamic_slice_in_dim(alpha_live, alpha_index * alpha_count, alpha_count, 0)
    my_source, tally = my_source.reshape(-1), jnp.sum(my_live, axis=1)

    def alpha_parts():
        gathered = lax.all_gather(coeffs, "alpha", axis=0, tiled=True)

        def alpha_step(target):
            return lambda total: alpha_call(target, my_source, tally, alpha_tiles, gathered, total)

        return [alpha_step(target) for target in range(alpha_count)]

    if beta_devices == DEVICES and beta_hamiltonian_tiles.shape[:2] == (8, 8):
        here = beta_index[None].astype(jnp.int32)
        plan = send_plan(here, source, live, *beta_hamiltonian_tiles.shape[:2])

        def branch(form):
            return lambda: line_of_four(
                form,
                plan,
                here,
                coeffs,
                diag,
                beta_hamiltonian_tiles,
                source,
                live,
                alpha_parts(),
            )

        form = plan[sizes(beta_hamiltonian_tiles.shape[0])[1]]
        return lax.switch(form, [branch(k) for k in range(len(FORMS))])
    alpha_steps = alpha_parts()

    rightward = [(j, j + 1) for j in range(beta_devices - 1)]
    leftward = [(j + 1, j) for j in range(beta_devices - 1)]
    pieces = [coeffs[h * half_rows : (h + 1) * half_rows] for h in range(HALVES)]
    arrived = []
    from_left, from_right = list(pieces), list(pieces)
    for _ in range(beta_devices - 1):
        for h in range(HALVES):
            from_left[h] = lax.ppermute(from_left[h], "beta", rightward)
            from_right[h] = lax.ppermute(from_right[h], "beta", leftward)
        arrived.append((list(from_left), list(from_right)))

    def place(step):
        return jnp.stack([beta_index, jnp.full((), step, beta_index.dtype)]).astype(jnp.int32)

    total = beta_call(
        source,
        live,
        place(0),
        beta_hamiltonian_tiles,
        (coeffs,),
        None,
        0,
        diag,
    )
    for step in range(1, beta_devices):
        if step == beta_devices - 1:
            for alpha in alpha_steps:
                total = alpha(total)
        lefts, rights = arrived[step - 1]
        for h in range(HALVES):
            total = beta_call(
                source,
                live,
                place(step),
                beta_hamiltonian_tiles,
                (lefts[h], rights[h]),
                total,
                h,
            )
    return total


def solution(mesh):
    return jax.shard_map(
        per_device,
        mesh=mesh,
        in_specs=(
            P("alpha", "beta"),
            P("alpha"),
            P("beta"),
            P("alpha", None, None, None),
            P("beta", None, None, None),
            P(),
            P(),
            P(),
            P(),
        ),
        out_specs=P("alpha", "beta"),
        check_vma=False,
    )
```

```python
import functools

import jax
import jax.numpy as jnp
from jax import lax
from jax.experimental import pallas as pl
from jax.experimental.pallas import tpu as pltpu
from jax.sharding import PartitionSpec as P

HALVES = 2
VMEM_LIMIT = 48 * 1024 * 1024


def split(x):
    high = x.astype(jnp.bfloat16)
    low = (x - high.astype(jnp.float32)).astype(jnp.bfloat16)
    return high, low


def product(a, b):
    a_high, a_low = a
    b_high, b_low = b
    dot = functools.partial(jnp.dot, preferred_element_type=jnp.float32)
    return dot(a_high, b_high) + (dot(a_high, b_low) + dot(a_low, b_high))


def beta_kernel(couplings, count, first, source, live, place, *refs):
    if first:
        tiles, da, db, own, out = refs
        buffers = (own,)
    else:
        tiles, left, right, total, out = refs
        buffers = (left, right)
    size = tiles.shape[-1]
    me, step = place[0], place[1]
    target = pl.program_id(0)
    if first:
        columns = pl.ds(pl.multiple_of(target * size, size), size)
        out[...] = (da[...] + db[:, columns]) * own[:, columns]
    else:
        out[...] = total[...]
    owners = (me,) if first else (me - step, me + step)

    def slot(c, carry):
        at = (me * count + target) * couplings + c
        block = source[at]
        owner = block // count
        inner = block - owner * count
        columns = pl.ds(pl.multiple_of(inner * size, size), size)
        for buffer, wanted in zip(buffers, owners):

            @pl.when(jnp.logical_and(live[at] != 0, owner == wanted))
            def _():
                out[...] += product(split(buffer[:, columns]), split(tiles[0, c]))

        return carry

    lax.fori_loop(0, couplings, slot, 0)


def beta_call(source, live, place, tiles, buffers, total, half, diag=None):
    count, couplings, size, _ = tiles.shape
    rows, cols = buffers[0].shape[0] // (HALVES if diag is not None else 1), buffers[0].shape[1]
    first = diag is not None
    once = pl.Buffered(buffer_count=1)
    tile_spec = pl.BlockSpec((1, couplings, size, size), lambda j, *_: (j, 0, 0, 0))
    out_spec = pl.BlockSpec((rows, size), lambda j, *_: (half, j))
    if first:
        rows = buffers[0].shape[0]
        out_spec = pl.BlockSpec((rows, size), lambda j, *_: (0, j))
        in_specs = [
            tile_spec,
            pl.BlockSpec((rows, 1), lambda j, *_: (0, 0), pipeline_mode=once),
            pl.BlockSpec((1, cols), lambda j, *_: (0, 0), pipeline_mode=once),
            pl.BlockSpec((rows, cols), lambda j, *_: (0, 0), pipeline_mode=once),
        ]
        operands = (tiles, *diag, *buffers)
        shape = buffers[0].shape
        aliases = {}
    else:
        whole = pl.BlockSpec((rows, cols), lambda j, *_: (0, 0), pipeline_mode=once)
        in_specs = [tile_spec, whole, whole, out_spec]
        operands = (tiles, *buffers, total)
        shape = total.shape
        aliases = {6: 0}
    return pl.pallas_call(
        functools.partial(beta_kernel, couplings, count, first),
        grid_spec=pltpu.PrefetchScalarGridSpec(
            num_scalar_prefetch=3,
            grid=(count,),
            in_specs=in_specs,
            out_specs=out_spec,
        ),
        out_shape=jax.ShapeDtypeStruct(shape, jnp.float32),
        input_output_aliases=aliases,
        compiler_params=pltpu.CompilerParams(vmem_limit_bytes=VMEM_LIMIT),
        cost_estimate=pl.CostEstimate(
            flops=6 * rows * cols * size * couplings // 2,
            bytes_accessed=4 * (tiles.size + 4 * rows * cols),
            transcendentals=0,
        ),
    )(source, live, place, *operands)


def alpha_kernel(target, couplings, chunk, source, tally, tiles, rows, total, out):
    c = pl.program_id(0)

    @pl.when(c == 0)
    def _():
        out[...] = total[...]

    @pl.when(c < tally[target])
    def _():
        tile = split(tiles[0, 0])

        def part(k, carry):
            columns = pl.ds(pl.multiple_of(k * chunk, chunk), chunk)
            out[:, columns] += product(tile, split(rows[:, columns]))
            return carry

        lax.fori_loop(0, out.shape[1] // chunk, part, 0)


def alpha_call(target, source, tally, tiles, gathered, total):
    _, couplings, size, _ = tiles.shape
    cols = total.shape[1]
    chunk = 256

    def last(c, tally):
        return jnp.minimum(c, tally[target] - 1)

    out_spec = pl.BlockSpec((size, cols), lambda c, s, t: (target, 0))
    return pl.pallas_call(
        functools.partial(alpha_kernel, target, couplings, chunk),
        grid_spec=pltpu.PrefetchScalarGridSpec(
            num_scalar_prefetch=2,
            grid=(couplings,),
            in_specs=[
                pl.BlockSpec((1, 1, size, size), lambda c, s, t: (target, last(c, t), 0, 0)),
                pl.BlockSpec(
                    (size, cols), lambda c, s, t: (s[target * couplings + last(c, t)], 0)
                ),
                out_spec,
            ],
            out_specs=out_spec,
        ),
        out_shape=jax.ShapeDtypeStruct(total.shape, jnp.float32),
        input_output_aliases={4: 0},
        compiler_params=pltpu.CompilerParams(vmem_limit_bytes=VMEM_LIMIT),
        cost_estimate=pl.CostEstimate(
            flops=6 * size * cols * size * couplings // 2,
            bytes_accessed=4 * size * cols * couplings,
            transcendentals=0,
        ),
    )(source, tally, tiles, gathered, total)


DEVICES = 4
PACKET = 2
PACKETS = 12
FORMS = ((2, 10), (1, 10), (1, 12))
AHEAD = 4
GROUPS = ((0, 0), (1, 4), (5, 6), (7, 9), (10, 10), (11, 12))


def sizes(blocks):
    others = (DEVICES - 1) * blocks
    flag = 2 * PACKETS * PACKET
    spot = flag + 1
    return others, flag, spot, spot + 2 * others


def send_plan_kernel(blocks, couplings, place, source, live, out, need, order, before):
    others, flag, spot, _ = sizes(blocks)
    me = place[0]
    requests = blocks * couplings
    counts = []
    for way in range(2):
        end = DEVICES - 1 if way == 0 else 0
        base = way * others
        base_before = way * (others + 1)

        def clear(u, carry):
            need[base + u] = 0
            order[base + u] = 0
            out[spot + base + u] = 0
            return carry

        lax.fori_loop(0, others, clear, 0)

        def mark(q, carry):
            block = source[end * requests + q]
            owner = block // blocks
            far = end - owner if way == 0 else owner - end

            @pl.when(jnp.logical_and(live[end * requests + q] != 0, far > 0))
            def _():
                need[base + (far - 1) * blocks + block - owner * blocks] = 1

            return carry

        lax.fori_loop(0, requests, mark, 0)

        def number(u, k):
            before[base_before + u] = k

            @pl.when(need[base + u] != 0)
            def _():
                order[base + k] = u

            return k + need[base + u]

        asked = lax.fori_loop(0, others, number, 0)
        before[base_before + others] = asked
        counts.append(asked)
    most = jnp.maximum(*counts)
    fits = [PACKET * (stop - start + 1) for start, stop in FORMS]
    form = (most > fits[0]).astype(jnp.int32) + (most > fits[1]).astype(jnp.int32)
    out[flag] = form
    for way in range(2):
        last = DEVICES - 2 if way == 0 else 1
        base = way * others
        base_before = way * (others + 1)
        sent = jnp.int32(0)
        for p in range(1, PACKETS + 1):
            ready = before[base_before + min(others, blocks + PACKET * max(0, p - 2))]
            if p < FORMS[0][0]:
                ready = jnp.where(form == 0, 0, ready)
            after = jnp.minimum(sent + PACKET, ready)
            for s in range(PACKET):
                used = sent + s < after
                u = order[base + jnp.minimum(sent + s, others - 1)]
                plain = PACKET * (p - 1) + s if p <= 2 * blocks // PACKET else s
                out[(way * PACKETS + p - 1) * PACKET + s] = jnp.where(
                    me == last, jnp.where(used, u, s), plain
                )

                @pl.when(used)
                def _():
                    out[spot + base + u] = p * PACKET + s

            sent = after


def send_plan(place, source, live, blocks, couplings):
    others, _, _, length = sizes(blocks)
    smem = pl.BlockSpec(memory_space=pltpu.SMEM)
    return pl.pallas_call(
        functools.partial(send_plan_kernel, blocks, couplings),
        in_specs=[smem] * 3,
        out_specs=smem,
        out_shape=jax.ShapeDtypeStruct((length,), jnp.int32),
        scratch_shapes=[
            pltpu.SMEM((2 * others,), jnp.int32),
            pltpu.SMEM((2 * others,), jnp.int32),
            pltpu.SMEM((2 * (others + 1),), jnp.int32),
        ],
    )(place, source, live)


def work_plan_kernel(blocks, couplings, place, plan, source, live, after, out, packet, buffer):
    others, _, spot, _ = sizes(blocks)
    me = place[0]
    requests = blocks * couplings
    base = len(GROUPS) * (blocks + 1)

    def locate(q, carry):
        block = source[me * requests + q]
        owner = block // blocks
        inner = block - owner * blocks
        way = jnp.where(owner < me, 0, 1)
        far = jnp.abs(owner - me)
        at_end = me == jnp.where(owner < me, DEVICES - 1, 0)
        u = jnp.maximum((far - 1) * blocks + inner, 0)
        ended = plan[spot + way * others + u]
        p = jnp.where(at_end, ended // PACKET, u // PACKET + 1)
        s = jnp.where(at_end, ended % PACKET, u % PACKET)
        own = owner == me
        packet[q] = jnp.where(live[me * requests + q] == 0, -1, jnp.where(own, 0, p))
        buffer[q] = jnp.where(own, inner, way * PACKET + s)
        return carry

    lax.fori_loop(0, requests, locate, 0)
    filled = jnp.int32(0)
    for g, (low, high) in enumerate(GROUPS):

        def target(j, filled):
            out[g * (blocks + 1) + j] = filled

            def slot(c, filled):
                q = j * couplings + c
                p = packet[q]
                mine = jnp.logical_and(p >= low, p <= high)

                @pl.when(mine)
                def _():
                    out[base + filled] = q * 256 + (p - low) * 2 * PACKET + buffer[q]

                return filled + mine.astype(jnp.int32)

            return lax.fori_loop(0, couplings, slot, filled)

        filled = lax.fori_loop(0, blocks, target, filled)
        out[g * (blocks + 1) + blocks] = filled


def work_plan(place, plan, source, live, blocks, couplings, after):
    requests = blocks * couplings
    smem = pl.BlockSpec(memory_space=pltpu.SMEM)
    return pl.pallas_call(
        functools.partial(work_plan_kernel, blocks, couplings),
        in_specs=[smem] * 4 + [pl.BlockSpec(memory_space=pl.ANY)],
        out_specs=smem,
        out_shape=jax.ShapeDtypeStruct(
            (len(GROUPS) * (blocks + 1) + requests,), jnp.int32
        ),
        scratch_shapes=[pltpu.SMEM((requests,), jnp.int32)] * 2,
    )(place, plan, source, live, after)


def pack_kernel(p, blocks, size, held, plan, *refs):
    own = refs[0]
    pool = (refs[1 : 1 + held], refs[1 + held : 1 + 2 * held])
    outs, sems = refs[-3:-1], refs[-1]
    width = outs[0].shape[0]
    for way in range(2):
        for s in range(width):
            u = plan[(way * PACKETS + p - 1) * PACKET + s]

            @pl.when(u < blocks)
            def _():
                columns = pl.ds(pl.multiple_of(u * size, size), size)
                pltpu.make_async_copy(
                    own.at[:, columns], outs[way].at[s], sems.at[way, s]
                ).start()

            for r in range(held):

                @pl.when(jnp.logical_and(u >= blocks, (u - blocks) // PACKET == r))
                def _():
                    pltpu.make_async_copy(
                        pool[way][r].at[(u - blocks) % PACKET], outs[way].at[s], sems.at[way, s]
                    ).start()

    for way in range(2):
        for s in range(width):
            pltpu.make_async_copy(
                outs[way].at[s], outs[way].at[s], sems.at[way, s]
            ).wait()


def pack(p, plan, coeffs, came, blocks, after):
    held = max(0, min(p - 2, 2 * blocks // PACKET))
    rows, cols = coeffs.shape
    size = cols // blocks
    width = PACKET
    any_spec = pl.BlockSpec(memory_space=pl.ANY)
    inputs = [coeffs] + [right for right, _ in came[:held]] + [left for _, left in came[:held]]
    inputs += after
    return pl.pallas_call(
        functools.partial(pack_kernel, p, blocks, size, held),
        grid_spec=pltpu.PrefetchScalarGridSpec(
            num_scalar_prefetch=1,
            grid=(1,),
            in_specs=[any_spec] * len(inputs),
            out_specs=[pl.BlockSpec((width, rows, size), lambda i, *_: (0, 0, 0))] * 2,
            scratch_shapes=[pltpu.SemaphoreType.DMA((2, width))],
        ),
        out_shape=[jax.ShapeDtypeStruct((width, rows, size), jnp.float32)] * 2,
        compiler_params=pltpu.CompilerParams(vmem_limit_bytes=VMEM_LIMIT),
        cost_estimate=pl.CostEstimate(
            flops=0, bytes_accessed=16 * width * rows * size, transcendentals=0
        ),
    )(plan, *inputs)


def work_kernel(g, blocks, couplings, size, held, work, *refs):
    base = len(GROUPS) * (blocks + 1)
    tiles, sources = refs[0], refs[1 : 1 + held]
    out, block_slots, tile_slots, sems = refs[-4:]
    target = pl.program_id(0)
    first, stop = work[g * (blocks + 1)], work[g * (blocks + 1) + blocks]

    def fetch(e):
        slot = e % AHEAD
        entry = work[base + e]
        where = entry % 256
        pltpu.make_async_copy(
            tiles.at[entry // 256], tile_slots.at[slot], sems.at[0, slot]
        ).start()
        if g == 0:
            columns = pl.ds(pl.multiple_of(where * size, size), size)
            pltpu.make_async_copy(
                sources[0].at[:, columns], block_slots.at[slot], sems.at[1, slot]
            ).start()
        else:
            for i in range(held):

                @pl.when(where // PACKET == i)
                def _():
                    pltpu.make_async_copy(
                        sources[i].at[where % PACKET], block_slots.at[slot], sems.at[1, slot]
                    ).start()

    @pl.when(target == 0)
    def _():
        for i in range(AHEAD - 1):

            @pl.when(first + i < stop)
            def _():
                fetch(first + i)

    if g == 0:
        da, db, mine = refs[1 + held : 4 + held]
        out[...] = (da[...] + db[...]) * mine[...]
    else:
        out[...] = refs[1 + held][...]

    def entry(e, carry):
        @pl.when(e + AHEAD - 1 < stop)
        def _():
            fetch(e + AHEAD - 1)

        slot = e % AHEAD
        pltpu.make_async_copy(tiles.at[0], tile_slots.at[slot], sems.at[0, slot]).wait()
        pltpu.make_async_copy(
            block_slots.at[slot], block_slots.at[slot], sems.at[1, slot]
        ).wait()
        tile = split(tile_slots[slot])
        half = out.shape[0] // HALVES
        for h in range(HALVES):
            rows = pl.ds(h * half, half)
            out[rows, :] += product(split(block_slots[slot, rows, :]), tile)
        return carry

    at = g * (blocks + 1) + target
    lax.fori_loop(work[at], work[at + 1], entry, 0)


def work_call(g, work, tiles, sources, rest, after):
    blocks, couplings, size, _ = tiles.shape
    rows, cols = rest[-1].shape
    low, high = GROUPS[g]
    any_spec = pl.BlockSpec(memory_space=pl.ANY)
    column = pl.BlockSpec((rows, size), lambda j, *_: (0, j))
    specs = [column]
    if g == 0:
        specs = [
            pl.BlockSpec((rows, 1), lambda j, *_: (0, 0)),
            pl.BlockSpec((1, size), lambda j, *_: (0, j)),
            column,
        ]
    held = len(sources)
    return pl.pallas_call(
        functools.partial(work_kernel, g, blocks, couplings, size, held),
        grid_spec=pltpu.PrefetchScalarGridSpec(
            num_scalar_prefetch=1,
            grid=(blocks,),
            in_specs=[any_spec] * (1 + held) + specs + [any_spec] * len(after),
            out_specs=column,
            scratch_shapes=[
                pltpu.VMEM((AHEAD, rows, size), jnp.float32),
                pltpu.VMEM((AHEAD, size, size), jnp.float32),
                pltpu.SemaphoreType.DMA((2, AHEAD)),
            ],
        ),
        out_shape=jax.ShapeDtypeStruct((rows, cols), jnp.float32),
        input_output_aliases={} if g == 0 else {2 + held: 0},
        compiler_params=pltpu.CompilerParams(vmem_limit_bytes=VMEM_LIMIT),
        cost_estimate=pl.CostEstimate(
            flops=6 * rows * cols * size * couplings // 8,
            bytes_accessed=8 * rows * cols,
            transcendentals=0,
        ),
    )(work, tiles.reshape(blocks * couplings, size, size), *sources, *rest, *after)


def line_of_four(form, plan, place, coeffs, diag, beta_tiles, source, live, alpha_steps):
    blocks, couplings, _, _ = beta_tiles.shape
    start, packets = FORMS[form]
    half = 2 * blocks // PACKET
    came = []

    def send(p, after):
        right, left = pack(p, plan, coeffs, came, blocks, after)
        links = [(j, j + 1) for j in range(DEVICES - 1)]
        links = links[0 if p <= half // 2 else 1 if p <= half else 2 :]
        if p < start:
            links = links[:-1]
        right_in = lax.ppermute(right, "beta", links)
        left_in = lax.ppermute(
            left, "beta", [(DEVICES - 1 - a, DEVICES - 1 - b) for a, b in links]
        )
        return (right_in, left_in), right

    def add(g, total, packed):
        low, high = GROUPS[g]
        buffers = [buffer for pair in came[low - 1 : high] for buffer in pair]
        return work_call(g, work, beta_tiles, buffers, [total], [packed])

    total = None
    for p in range(1, packets + 1):
        arriving, packed = send(p, [] if total is None else [total])
        came.append(arriving)
        if p == 2:
            work = work_plan(place, plan, source, live, blocks, couplings, packed)
            total = work_call(0, work, beta_tiles, [coeffs], [*diag, coeffs], [packed])
        elif p == 6:
            total = add(1, total, packed)
        elif p == 8:
            total = add(2, total, packed)
        elif p == 9:
            total = alpha_steps[0](total)
        elif p == 10:
            for step in alpha_steps[1:]:
                total = step(total)
        elif p == 11:
            total = add(3, total, packed)
    if packets <= 10:
        total = add(3, total, packed)
    total = add(4, total, packed)
    return add(5, total, packed) if packets > 10 else total


def per_device(
    coeffs,
    diag_alpha,
    diag_beta,
    alpha_tiles,
    beta_hamiltonian_tiles,
    alpha_source,
    alpha_live,
    beta_source_block,
    beta_live,
):
    rows = coeffs.shape[0]
    alpha_count = alpha_tiles.shape[0]
    beta_devices = lax.axis_size("beta")
    alpha_index = lax.axis_index("alpha")
    beta_index = lax.axis_index("beta")
    half_rows = rows // HALVES
    source = beta_source_block.reshape(-1)
    live = beta_live.reshape(-1)
    diag = (diag_alpha[:, None], diag_beta[None, :])
    my_source = lax.dynamic_slice_in_dim(alpha_source, alpha_index * alpha_count, alpha_count, 0)
    my_live = lax.dynamic_slice_in_dim(alpha_live, alpha_index * alpha_count, alpha_count, 0)
    my_source, tally = my_source.reshape(-1), jnp.sum(my_live, axis=1)

    def alpha_parts():
        gathered = lax.all_gather(coeffs, "alpha", axis=0, tiled=True)

        def alpha_step(target):
            return lambda total: alpha_call(target, my_source, tally, alpha_tiles, gathered, total)

        return [alpha_step(target) for target in range(alpha_count)]

    if beta_devices == DEVICES and beta_hamiltonian_tiles.shape[:2] == (8, 8):
        here = beta_index[None].astype(jnp.int32)
        plan = send_plan(here, source, live, *beta_hamiltonian_tiles.shape[:2])

        def branch(form):
            return lambda: line_of_four(
                form,
                plan,
                here,
                coeffs,
                diag,
                beta_hamiltonian_tiles,
                source,
                live,
                alpha_parts(),
            )

        form = plan[sizes(beta_hamiltonian_tiles.shape[0])[1]]
        return lax.switch(form, [branch(k) for k in range(len(FORMS))])
    alpha_steps = alpha_parts()

    rightward = [(j, j + 1) for j in range(beta_devices - 1)]
    leftward = [(j + 1, j) for j in range(beta_devices - 1)]
    pieces = [coeffs[h * half_rows : (h + 1) * half_rows] for h in range(HALVES)]
    arrived = []
    from_left, from_right = list(pieces), list(pieces)
    for _ in range(beta_devices - 1):
        for h in range(HALVES):
            from_left[h] = lax.ppermute(from_left[h], "beta", rightward)
            from_right[h] = lax.ppermute(from_right[h], "beta", leftward)
        arrived.append((list(from_left), list(from_right)))

    def place(step):
        return jnp.stack([beta_index, jnp.full((), step, beta_index.dtype)]).astype(jnp.int32)

    total = beta_call(
        source,
        live,
        place(0),
        beta_hamiltonian_tiles,
        (coeffs,),
        None,
        0,
        diag,
    )
    for step in range(1, beta_devices):
        if step == beta_devices - 1:
            for alpha in alpha_steps:
                total = alpha(total)
        lefts, rights = arrived[step - 1]
        for h in range(HALVES):
            total = beta_call(
                source,
                live,
                place(step),
                beta_hamiltonian_tiles,
                (lefts[h], rights[h]),
                total,
                h,
            )
    return total


def solution(mesh):
    return jax.shard_map(
        per_device,
        mesh=mesh,
        in_specs=(
            P("alpha", "beta"),
            P("alpha"),
            P("beta"),
            P("alpha", None, None, None),
            P("beta", None, None, None),
            P(),
            P(),
            P(),
            P(),
        ),
        out_specs=P("alpha", "beta"),
        check_vma=False,
    )
```
